512 devices in a mesh: ctx: 128 (over z, x, y_lo, core), head: 4 (over y_hi).
Axes of the slice: x: 4, y: 8 (y_hi: 4, y_lo: 2; y = y_hi * 2 + y_lo), z: 8, core: 2. Of those that a mesh axis runs over, the one named last changes fastest.
Arguments:
- hidden: bfloat16 [10240, 2048], P('ctx'), may hold values from -6 to 6
- self_gain: float32 [2048], replicated, may hold values from 0.5 to 8, as said below
- cross_gain: float32 [2048], replicated, may hold values from 0.5 to 8, as said below
- self_query: bfloat16 [2048, 1024], P(None, 'head'), may hold values from -0.0625 to 0.0625
- self_key: bfloat16 [2048, 1024], P(None, 'head'), may hold values from -0.125 to 0.125
- self_value: bfloat16 [2048, 1024], P(None, 'head'), may hold values from -0.125 to 0.125
- self_out: bfloat16 [2048, 1024], P(None, 'head'), may hold values from -0.1875 to 0.1875
- cross_query: bfloat16 [2048, 1024], P('ctx', 'head'), may hold values from -0.0625 to 0.0625
- cross_out: bfloat16 [2048, 1024], P('ctx', 'head'), may hold values from -0.1875 to 0.1875
- enc_key: bfloat16 [2048, 1024], P('ctx', 'head'), may hold values from -6 to 6
- enc_value: bfloat16 [2048, 1024], P('ctx', 'head'), may hold values from -6 to 6
Outputs:
- layer_out: bfloat16 [10240, 2048], P('ctx', 'head')
The draws below stay inside these ranges and needn't reach their ends.
Inputs may be any that keep to these rules, and one draw needn't show every extreme that they name: `self_gain`: positive norm gains. `cross_gain`: positive norm gains.
All inputs are finite; a program needn't handle non-finite values.
Results may differ from the reference program's by a relative error of at most 0.03.
The reference program's roundings to bfloat16 on the way count: a program that leaves them out, or rounds other values in their place, can miss the bound.
Values may be sent and summed in bfloat16 or wider, within the bound.
A program may use at most 128 MiB of HBM per device.

```python
import jax
import jax.numpy as jnp
from jax import lax

D = 2048
KV = 64
HEADS = 16
DEC = 10240
ENC = 2048


def draw_self_gain(key, part):
    key = jax.random.fold_in(key, 11)
    return jax.random.uniform(key, (D,), jnp.float32, 0.5, 1.5)


def draw_cross_gain(key, part):
    key = jax.random.fold_in(key, 23)
    return jax.random.uniform(key, (D,), jnp.float32, 0.5, 1.5)


def steps_of(stream_key, dims, pieces, smallest, largest):
    def one(dim, parts):
        heights = jax.random.uniform(jax.random.fold_in(jax.random.fold_in(stream_key, 6), dim), (parts,), jnp.float32, smallest / len(pieces), largest / len(pieces))
        return jnp.repeat(jnp.exp(heights), dims[dim] // parts).reshape((-1,) + (1,) * (len(dims) - dim - 1))

    level = one(*pieces[0])
    for cut in pieces[1:]:
        level = level * one(*cut)
    return level


def bell_draw(own_key, shape, spread, bound, shards=(), held_as=jnp.bfloat16):
    result = spread * jax.random.normal(own_key, shape, jnp.float32)
    if shards:
        result = result * steps_of(own_key, shape, shards, -0.22, 0.18)
    return jnp.clip(result, -bound, bound).astype(held_as)


def setup_inputs(seed: int = 0) -> dict:
    seeds = jax.random.split(jax.random.key(seed), 12)
    hidden = bell_draw(seeds[0], (DEC, D), 1.0, 6.0, ((0, 128),))
    self_gain = draw_self_gain(jax.random.fold_in(seeds[11], 71), 0)
    cross_gain = draw_cross_gain(jax.random.fold_in(seeds[11], 71), 0)
    self_query = bell_draw(seeds[3], (D, HEADS * KV), (4 * D) ** -0.5, 0.0625, ((1, 4),))
    self_key = bell_draw(seeds[4], (D, HEADS * KV), D ** -0.5, 0.125, ((1, 4),))
    self_value = bell_draw(seeds[5], (D, HEADS * KV), D ** -0.5, 0.125, ((1, 4),))
    self_out = bell_draw(seeds[6], (D, HEADS * KV), (HEADS * KV) ** -0.5, 0.1875, ((1, 4),))
    cross_query = bell_draw(seeds[7], (D, HEADS * KV), (4 * D) ** -0.5, 0.0625, ((0, 128), (1, 4)))
    cross_out = bell_draw(seeds[8], (D, HEADS * KV), (HEADS * KV) ** -0.5, 0.1875, ((0, 128), (1, 4)))
    enc_key = bell_draw(seeds[9], (ENC, HEADS * KV), 1.0, 6.0, ((0, 128), (1, 4)))
    enc_value = bell_draw(seeds[10], (ENC, HEADS * KV), 1.0, 6.0, ((0, 128), (1, 4)))
    return {"hidden": hidden, "self_gain": self_gain, "cross_gain": cross_gain, "self_query": self_query, "self_key": self_key, "self_value": self_value, "self_out": self_out, "cross_query": cross_query, "cross_out": cross_out, "enc_key": enc_key, "enc_value": enc_value}


epsilon = 1e-06

def rms_scale(vector, gain_vector):
    mean_square = lax.optimization_barrier(jnp.mean(vector * vector, axis=-1, keepdims=True))
    return vector * lax.rsqrt(mean_square + epsilon) * gain_vector

def head_attention(queries, key_rows, value_rows, head_index, causal):
    offset = (head_index * KV).astype(jnp.int32)
    query_head = lax.dynamic_slice_in_dim(queries, offset, KV, 1)
    key_head = lax.dynamic_slice_in_dim(key_rows, offset, KV, 1)
    value_head = lax.dynamic_slice_in_dim(value_rows, offset, KV, 1)
    scores = jnp.dot(query_head, key_head.T, preferred_element_type=jnp.float32)
    if causal:
        positions = jnp.arange(scores.shape[0], dtype=jnp.int32)
        visible = positions[None, :] <= positions[:, None]
        scores = jnp.where(visible, scores, jnp.float32(-1e+30))
        peak_score = lax.optimization_barrier(jnp.max(scores, axis=1, keepdims=True))
        weights = jnp.where(visible, jnp.exp(scores - peak_score), jnp.float32(0.0))
    else:
        peak_score = lax.optimization_barrier(jnp.max(scores, axis=1, keepdims=True))
        weights = jnp.exp(scores - peak_score)
    weight_sum = lax.optimization_barrier(jnp.sum(weights, axis=1, keepdims=True))
    mixed_values = jnp.dot(weights.astype(jnp.bfloat16), value_head, preferred_element_type=jnp.float32)
    return mixed_values / weight_sum

def all_heads(queries, key_rows, value_rows, causal):
    per_head = lax.map(lambda head_index: head_attention(queries, key_rows, value_rows, head_index, causal), jnp.arange(HEADS, dtype=jnp.int32))
    return jnp.transpose(per_head, (1, 0, 2)).reshape(queries.shape[0], HEADS * KV).astype(jnp.bfloat16)

def reference(hidden, self_gain, cross_gain, self_query, self_key, self_value, self_out, cross_query, cross_out, enc_key, enc_value):
    inputs = hidden.astype(jnp.float32)
    normed = rms_scale(inputs, self_gain).astype(jnp.bfloat16)
    queries = jnp.dot(normed, self_query, preferred_element_type=jnp.float32).astype(jnp.bfloat16)
    key_rows = jnp.dot(normed, self_key, preferred_element_type=jnp.float32).astype(jnp.bfloat16)
    value_rows = jnp.dot(normed, self_value, preferred_element_type=jnp.float32).astype(jnp.bfloat16)
    attn_self = all_heads(queries, key_rows, value_rows, True)
    mixed_rows = inputs + jnp.dot(attn_self, self_out.T, preferred_element_type=jnp.float32)
    normed2 = rms_scale(mixed_rows, cross_gain).astype(jnp.bfloat16)
    cross_q = jnp.dot(normed2, cross_query, preferred_element_type=jnp.float32).astype(jnp.bfloat16)
    attn_cross = all_heads(cross_q, enc_key, enc_value, False)
    layer_out = mixed_rows + jnp.dot(attn_cross, cross_out.T, preferred_element_type=jnp.float32)
    return layer_out.astype(jnp.bfloat16)
```

```python
import functools

import jax
import jax.numpy as jnp
from jax import lax
from jax.experimental import pallas as pl
from jax.experimental.pallas import tpu as pltpu
from jax.sharding import PartitionSpec as P

KV = 64
CORES = 2
PLANE = 16
MESH = pl.DeviceIdType.MESH

epsilon = 1e-06

NT = (((1,), (1,)), ((), ()))
NN = (((1,), (0,)), ((), ()))


def matmul(left, right, dims=NN):
    return lax.dot_general(left, right, dims, preferred_element_type=jnp.float32)


def to_lanes(columns):
    rows = columns.shape[0]
    square = jnp.concatenate([columns, jnp.zeros((128 - rows, 128), jnp.float32)], axis=0)
    return jnp.transpose(square)[:8]


def to_columns(lanes, rows):
    square = jnp.concatenate([lanes, jnp.zeros((120, 128), jnp.float32)], axis=0)
    return jnp.transpose(square)[:rows]


def spread(per_head, width):
    rows = per_head.shape[0]
    owner = lax.broadcasted_iota(jnp.int32, (rows, width), 1) // KV
    result = jnp.zeros((rows, width), jnp.float32)
    for head in range(width // KV):
        result = jnp.where(owner == head, per_head[:, head : head + 1], result)
    return result


def attend(queries, keys, values, first_query):
    rows, width = queries.shape
    heads = width // KV
    owner = lax.broadcasted_iota(jnp.int32, (rows, width), 1) // KV
    zero = jnp.zeros_like(queries)
    stacked = jnp.concatenate(
        [jnp.where(owner == head, queries, zero) for head in range(heads)], axis=0
    )
    scores = matmul(stacked, keys, NT)
    if first_query is not None:
        token = lax.broadcasted_iota(jnp.int32, (rows, scores.shape[1]), 0) + first_query
        seen = lax.broadcasted_iota(jnp.int32, (rows, scores.shape[1]), 1) <= token
        scores = jnp.where(
            jnp.concatenate([seen] * heads, axis=0), scores, jnp.float32(-1e30)
        )
    peak = jnp.max(scores, axis=1, keepdims=True)
    weights = jnp.exp(scores - peak)
    total = jnp.sum(weights, axis=1, keepdims=True)
    mixed = matmul(weights.astype(jnp.bfloat16), values)
    mixed = mixed / total
    level = peak + jnp.log(total)
    result = jnp.zeros((rows, width), jnp.float32)
    levels = jnp.zeros((rows, 128), jnp.float32)
    column = lax.broadcasted_iota(jnp.int32, (rows, 128), 1)
    for head in range(heads):
        part = slice(head * rows, (head + 1) * rows)
        result = jnp.where(owner == head, mixed[part], result)
        levels = jnp.where(column == head, level[part], levels)
    return result, levels


def kernel(
    planes,
    plane_size,
    head_devices,
    hidden,
    self_gain,
    cross_gain,
    self_query,
    self_key,
    self_value,
    self_out,
    enc_key,
    enc_value,
    cross_query,
    cross_out,
    out,
    weights,
    normed,
    kv,
    qs,
    sent_part,
    sent_level,
    got_part,
    got_level,
    own_part,
    own_level,
    side,
    out_terms,
    got_terms,
    shares,
    squares,
    final_terms,
    got_final,
    load_sem,
    kv_send,
    kv_recv,
    side_z_send,
    side_z_recv,
    side_send,
    side_recv,
    q_send,
    q_recv,
    part_send,
    part_recv,
    level_send,
    level_recv,
    terms_send,
    terms_recv,
    share_send,
    share_recv,
    square_send,
    square_recv,
    final_send,
    final_recv,
):
    rows, width = hidden.shape
    share = width // head_devices
    chips = plane_size // CORES
    ctx = lax.axis_index("ctx")
    head = lax.axis_index("head")
    plane = ctx // plane_size
    place = ctx % plane_size
    chip = place // CORES
    core = place % CORES
    sibling_place = chip * CORES + (1 - core)

    def in_plane(other_place):
        return (plane * plane_size + other_place, head)

    def on_line(other_plane):
        return (other_plane * plane_size + place, head)

    def chip_place(step):
        return ((chip + step) % chips) * CORES + core

    def line_plane(step):
        return (plane + step) % planes

    def head_at(step):
        return (head + step) % head_devices

    def remote(src, dst, send, recv, device):
        return pltpu.make_async_remote_copy(
            src_ref=src,
            dst_ref=dst,
            send_sem=send,
            recv_sem=recv,
            device_id=device,
            device_id_type=MESH,
        )

    def each(low, high, step_fn):
        def step(index, carry):
            step_fn(index)
            return carry

        lax.fori_loop(low, high, step, 0)

    barrier = pltpu.get_barrier_semaphore()

    def greet(device):
        pl.semaphore_signal(barrier, inc=1, device_id=device, device_id_type=MESH)

    each(1, chips, lambda step: greet(in_plane(chip_place(step))))
    greet(in_plane(sibling_place))
    each(1, planes, lambda step: greet(on_line(line_plane(step))))
    each(1, head_devices, lambda step: greet((ctx, head_at(step))))

    loads = [
        pltpu.make_async_copy(source, weights.at[index], load_sem.at[index])
        for index, source in enumerate((self_key, self_value, self_query, self_out))
    ]
    for load in loads:
        load.start()
    for index, source in enumerate((enc_key, enc_value, cross_query, cross_out)):
        side[index, plane, place] = source[...]

    pl.semaphore_wait(barrier, (chips - 1) + 1 + (planes - 1) + (head_devices - 1))

    def side_line(step, other):
        block = side.at[:, other, place]
        return remote(
            block, block, side_z_send.at[step], side_z_recv.at[other], on_line(line_plane(step))
        )

    each(1, planes, lambda step: side_line(step, plane).start())

    inputs = hidden[...].astype(jnp.float32)
    mean_square = jnp.mean(inputs * inputs, axis=1, keepdims=True)
    normed[...] = (inputs * lax.rsqrt(mean_square + epsilon) * self_gain[...]).astype(jnp.bfloat16)

    for index in range(2):
        loads[index].wait()
        kv[index, place] = matmul(normed[...], weights[index]).astype(jnp.bfloat16)

    def spread_copy(buffer, send, recv):
        def copy(slot, sender, device):
            return remote(buffer(slot), buffer(slot), send.at[sender], recv.at[slot], device)

        def start():
            each(1, chips, lambda step: copy(place, step, in_plane(chip_place(step))).start())
            copy(place, 0, in_plane(sibling_place)).start()

        def forward():
            def one(step):
                slot = chip_place(step)
                copy(slot, chips + step, in_plane(sibling_place)).wait_recv()
                copy(slot, chips + step, in_plane(sibling_place)).start()

            each(1, chips, one)

        def finish():
            def one(step):
                slot = ((chip + step) % chips) * CORES + (1 - core)
                copy(slot, 0, in_plane(sibling_place)).wait_recv()

            each(0, chips, one)

        def drain():
            def one(step):
                copy(place, step, in_plane(sibling_place)).wait_send()

            each(0, chips, one)
            each(chips + 1, 2 * chips, one)

        return start, forward, finish, drain

    kv_start, kv_forward, kv_finish, kv_drain = spread_copy(
        lambda slot: kv.at[:, slot], kv_send, kv_recv
    )
    side_start, side_forward, side_finish, side_drain = spread_copy(
        lambda slot: side.at[:, :, slot], side_send, side_recv
    )
    kv_start()

    loads[2].wait()
    qs[plane] = matmul(normed[...], weights[2]).astype(jnp.bfloat16)

    def query_copy(source_plane, target_plane):
        return remote(
            qs.at[source_plane],
            qs.at[source_plane],
            q_send.at[target_plane],
            q_recv.at[source_plane],
            on_line(target_plane),
        )

    each(0, plane, lambda target: query_copy(plane, target).start())

    def side_arrival(step):
        side_line(step, line_plane(step)).wait_recv()

    each(1, planes, side_arrival)
    side_start()

    kv_forward()
    kv_finish()

    key_count = plane_size * rows
    hc = qs.shape[2]

    def plane_keys():
        return kv[0].reshape(key_count, hc), kv[1].reshape(key_count, hc)

    def part_copy(source_plane, target_plane):
        return remote(
            sent_part.at[target_plane],
            got_part.at[source_plane],
            part_send.at[target_plane],
            part_recv.at[source_plane],
            on_line(target_plane),
        )

    def level_copy(source_plane, target_plane):
        return remote(
            sent_level.at[target_plane],
            got_level.at[source_plane],
            level_send.at[target_plane],
            level_recv.at[source_plane],
            on_line(target_plane),
        )

    def later_plane(other):
        query_copy(other, plane).wait_recv()
        keys, values = plane_keys()
        part, levels = attend(qs[other], keys, values, None)
        sent_part[other] = part.astype(jnp.bfloat16)
        sent_level[other] = to_lanes(levels)
        part_copy(plane, other).start()
        level_copy(plane, other).start()

    each(plane + 1, planes, later_plane)
    keys, values = plane_keys()
    part, levels = attend(qs[plane], keys, values, place * rows)
    own_part[...] = part
    own_level[...] = levels

    side_forward()

    def join(other, state):
        mixed, peak, total = state
        part_copy(other, plane).wait_recv()
        level_copy(other, plane).wait_recv()
        level = to_columns(got_level[other], rows)
        new_peak = jnp.maximum(peak, level)
        keep = jnp.exp(peak - new_peak)
        add = jnp.exp(level - new_peak)
        mixed = mixed * spread(keep, hc) + got_part[other].astype(jnp.float32) * spread(add, hc)
        return mixed, new_peak, total * keep + add

    mixed, _, total = lax.fori_loop(
        0, plane, join, (own_part[...], own_level[...], jnp.ones((rows, 128), jnp.float32))
    )
    attn_self = (mixed / spread(total, hc)).astype(jnp.bfloat16)

    def exchange(source, target, send, recv):
        def copy(step):
            other = head_at(step)
            return remote(
                source(other), target(head), send.at[other], recv.at[head], (ctx, other)
            )

        def arrival(step):
            other = head_at(step)
            return remote(
                source(other), target(other), send.at[other], recv.at[other], (ctx, other)
            )

        def start():
            each(1, head_devices, lambda step: copy(step).start())

        def finish():
            each(1, head_devices, lambda step: arrival(step).wait_recv())

        def drain():
            each(1, head_devices, lambda step: copy(step).wait_send())

        return start, finish, drain

    loads[3].wait()
    terms_start, terms_finish, terms_drain = exchange(
        lambda other: out_terms.at[other], lambda slot: got_terms.at[slot], terms_send, terms_recv
    )
    for index in range(head_devices):
        out_terms[index] = matmul(
            attn_self, weights[3, index * share : (index + 1) * share], NT
        ).astype(jnp.bfloat16)
    terms_start()
    terms_finish()
    columns = pl.ds(pl.multiple_of(head * share, share), share)
    mixed_rows = hidden[:, columns].astype(jnp.float32) + out_terms[head].astype(jnp.float32)
    for step in range(1, head_devices):
        mixed_rows = mixed_rows + got_terms[head_at(step)].astype(jnp.float32)

    shares[head] = (mixed_rows * cross_gain[:, columns]).astype(jnp.bfloat16)
    square = jnp.sum(mixed_rows * mixed_rows, axis=1, keepdims=True)
    squares[head] = to_lanes(jnp.broadcast_to(square, (rows, 128)))
    share_start, share_finish, share_drain = exchange(
        lambda other: shares.at[head], lambda slot: shares.at[slot], share_send, share_recv
    )
    square_start, square_finish, square_drain = exchange(
        lambda other: squares.at[head], lambda slot: squares.at[slot], square_send, square_recv
    )
    square_start()
    share_start()

    side_finish()
    side_rows = planes * plane_size * side.shape[3]

    square_finish()
    share_finish()
    all_squares = squares[0]
    for index in range(1, head_devices):
        all_squares = all_squares + squares[index]
    scale = lax.rsqrt(to_columns(all_squares, rows)[:, :1] / width + epsilon)
    query_weights = side[2].reshape(side_rows, hc)
    cross_q = jnp.zeros((rows, hc), jnp.float32)
    for index in range(head_devices):
        cross_q = cross_q + matmul(
            shares[index], query_weights[index * share : (index + 1) * share]
        )
    cross_q = (cross_q * scale).astype(jnp.bfloat16)
    attn_cross, _ = attend(
        cross_q, side[0].reshape(side_rows, hc), side[1].reshape(side_rows, hc), None
    )
    attn_cross = attn_cross.astype(jnp.bfloat16)
    out_weights = side[3].reshape(side_rows, hc)
    for index in range(head_devices):
        final_terms[index] = matmul(
            attn_cross, out_weights[index * share : (index + 1) * share], NT
        ).astype(jnp.bfloat16)
    final_start, final_finish, final_drain = exchange(
        lambda other: final_terms.at[other], lambda slot: got_final.at[slot], final_send, final_recv
    )
    final_start()
    final_finish()
    result = mixed_rows + final_terms[head].astype(jnp.float32)
    for step in range(1, head_devices):
        result = result + got_final[head_at(step)].astype(jnp.float32)
    out[...] = result.astype(jnp.bfloat16)

    each(1, planes, lambda step: side_line(step, plane).wait_send())
    kv_drain()
    side_drain()
    each(0, plane, lambda target: query_copy(plane, target).wait_send())
    each(plane + 1, planes, lambda other: part_copy(plane, other).wait_send())
    each(plane + 1, planes, lambda other: level_copy(plane, other).wait_send())
    terms_drain()
    share_drain()
    square_drain()
    final_drain()


def body(
    plane_size,
    hidden,
    self_gain,
    cross_gain,
    self_query,
    self_key,
    self_value,
    self_out,
    cross_query,
    cross_out,
    enc_key,
    enc_value,
):
    rows, width = hidden.shape
    hc = self_query.shape[1]
    ctx_devices = lax.axis_size("ctx")
    head_devices = lax.axis_size("head")
    planes = ctx_devices // plane_size
    chips = plane_size // CORES
    share = width // head_devices
    piece = enc_key.shape[0]
    low, full = jnp.bfloat16, jnp.float32
    vmem = pl.BlockSpec(memory_space=pltpu.VMEM)
    hbm = pl.BlockSpec(memory_space=pl.ANY)
    dma = pltpu.SemaphoreType.DMA
    return pl.pallas_call(
        functools.partial(kernel, planes, plane_size, head_devices),
        out_shape=jax.ShapeDtypeStruct((rows, share), low),
        in_specs=[vmem] * 3 + [hbm] * 4 + [vmem] * 4,
        out_specs=vmem,
        scratch_shapes=[
            pltpu.VMEM((4, width, hc), low),
            pltpu.VMEM((rows, width), low),
            pltpu.VMEM((2, plane_size, rows, hc), low),
            pltpu.VMEM((planes, rows, hc), low),
            pltpu.VMEM((planes, rows, hc), low),
            pltpu.VMEM((planes, 8, 128), full),
            pltpu.VMEM((planes, rows, hc), low),
            pltpu.VMEM((planes, 8, 128), full),
            pltpu.VMEM((rows, hc), full),
            pltpu.VMEM((rows, 128), full),
            pltpu.VMEM((4, planes, plane_size, piece, hc), low),
            pltpu.VMEM((head_devices, rows, share), low),
            pltpu.VMEM((head_devices, rows, share), low),
            pltpu.VMEM((head_devices, rows, share), low),
            pltpu.VMEM((head_devices, 8, 128), full),
            pltpu.VMEM((head_devices, rows, share), low),
            pltpu.VMEM((head_devices, rows, share), low),
            dma((4,)),
            dma((2 * chips,)),
            dma((plane_size,)),
            dma((planes,)),
            dma((planes,)),
            dma((2 * chips,)),
            dma((plane_size,)),
        ]
        + [dma((planes,))] * 6
        + [dma((head_devices,))] * 8,
        compiler_params=pltpu.CompilerParams(
            collective_id=0, has_side_effects=True, vmem_limit_bytes=48 * 1024 * 1024
        ),
    )(
        hidden,
        self_gain.reshape(1, width),
        cross_gain.reshape(1, width),
        self_query,
        self_key,
        self_value,
        self_out,
        enc_key,
        enc_value,
        cross_query,
        cross_out,
    )


def solution(mesh, plane_size=PLANE):
    placed = (
        P("ctx", None),
        P(),
        P(),
        P(None, "head"),
        P(None, "head"),
        P(None, "head"),
        P(None, "head"),
        P("ctx", "head"),
        P("ctx", "head"),
        P("ctx", "head"),
        P("ctx", "head"),
    )
    return jax.shard_map(
        functools.partial(body, plane_size),
        mesh=mesh,
        in_specs=placed,
        out_specs=P("ctx", "head"),
        check_vma=False,
    )
```

```python
import functools

import jax
import jax.numpy as jnp
from jax import lax
from jax.experimental import pallas as pl
from jax.experimental.pallas import tpu as pltpu
from jax.sharding import PartitionSpec as P

KV = 64
PLANE = 16
VMEM_BYTES = 62 * 1024 * 1024
MESH = pl.DeviceIdType.MESH

epsilon = 1e-06

NT = (((1,), (1,)), ((), ()))
NN = (((1,), (0,)), ((), ()))


def matmul(left, right, dims=NN):
    return lax.dot_general(left, right, dims, preferred_element_type=jnp.float32)


def to_lanes(columns):
    rows = columns.shape[0]
    square = jnp.concatenate([columns, jnp.zeros((128 - rows, 128), jnp.float32)], axis=0)
    return jnp.transpose(square)[:8]


def to_columns(lanes, rows):
    square = jnp.concatenate([lanes, jnp.zeros((120, 128), jnp.float32)], axis=0)
    return jnp.transpose(square)[:rows]


def spread(per_head, width):
    rows = per_head.shape[0]
    owner = lax.broadcasted_iota(jnp.int32, (rows, width), 1) // KV
    result = jnp.zeros((rows, width), jnp.float32)
    for head in range(width // KV):
        result = jnp.where(owner == head, per_head[:, head : head + 1], result)
    return result


def attend(queries, keys, values, first_query):
    rows, width = queries.shape
    heads = width // KV
    owner = lax.broadcasted_iota(jnp.int32, (rows, width), 1) // KV
    zero = jnp.zeros_like(queries)
    stacked = jnp.concatenate(
        [jnp.where(owner == head, queries, zero) for head in range(heads)], axis=0
    )
    scores = matmul(stacked, keys, NT)
    if first_query is not None:
        token = lax.broadcasted_iota(jnp.int32, (rows, scores.shape[1]), 0) + first_query
        seen = lax.broadcasted_iota(jnp.int32, (rows, scores.shape[1]), 1) <= token
        scores = jnp.where(
            jnp.concatenate([seen] * heads, axis=0), scores, jnp.float32(-1e30)
        )
    peak = jnp.max(scores, axis=1, keepdims=True)
    weights = jnp.exp(scores - peak)
    total = jnp.sum(weights, axis=1, keepdims=True)
    mixed = matmul(weights.astype(jnp.bfloat16), values)
    mixed = mixed / total
    level = peak + jnp.log(total)
    result = jnp.zeros((rows, width), jnp.float32)
    levels = jnp.zeros((rows, 128), jnp.float32)
    column = lax.broadcasted_iota(jnp.int32, (rows, 128), 1)
    for head in range(heads):
        part = slice(head * rows, (head + 1) * rows)
        result = jnp.where(owner == head, mixed[part], result)
        levels = jnp.where(column == head, level[part], levels)
    return result, levels


def place_gather(buffer, send, recv, position, sizes, device_of):
    x, l, core = position
    x_size, device_count = sizes
    own = x * 4 + l * 2 + core
    across = x * 4 + (1 - l) * 2 + core
    sibling = device_of(x * 4 + l * 2 + 1 - core)
    partner = device_of(across)

    def slot_at(step, pair):
        return lax.rem(x + step, x_size) * 4 + pair * 2 + core

    def copy(slot, sender, device):
        return pltpu.make_async_remote_copy(
            src_ref=buffer(slot),
            dst_ref=buffer(slot),
            send_sem=send.at[sender],
            recv_sem=recv.at[slot],
            device_id=device,
            device_id_type=MESH,
        )

    def arrived(slot):
        copy(slot, 0, sibling).wait_recv()

    def to_sibling(slot, sender):
        copy(slot, sender, sibling).start()

    def to_partner(slot, sender):
        copy(slot, sender, partner).start()

    def to_line(slot, sender):
        each(1, x_size, lambda step: copy(slot, sender + step, device_of(slot_at(step, l))).start())

    def finish():
        each(0, device_count // 2, lambda step: arrived(step * 2 + 1 - core))

    class Pair:
        @staticmethod
        def start():
            to_partner(own, 0)
            to_sibling(own, 1)

        @staticmethod
        def start_line():
            to_line(own, 1)

        @staticmethod
        def middle():
            arrived(across)
            to_line(across, x_size)
            to_sibling(across, 2 * x_size)

        @staticmethod
        def forward():
            def one(step):
                arrived(slot_at(step, l))
                to_sibling(slot_at(step, l), 2 * x_size + step)

            each(1, x_size, one)

        @staticmethod
        def forward_across():
            def one(step):
                arrived(slot_at(step, 1 - l))
                to_sibling(slot_at(step, 1 - l), 3 * x_size - 1 + step)

            each(1, x_size, one)

    class Line:
        @staticmethod
        def start():
            to_line(own, -1)
            to_partner(own, x_size - 1)
            to_sibling(own, x_size)

        @staticmethod
        def forward():
            def one(step):
                arrived(slot_at(step, l))
                to_partner(slot_at(step, l), x_size + step)
                to_sibling(slot_at(step, l), 2 * x_size - 1 + step)

            each(1, x_size, one)

        @staticmethod
        def forward_across():
            def one(step):
                arrived(slot_at(step, 1 - l))
                to_sibling(slot_at(step, 1 - l), 3 * x_size - 1 + step)

            each(0, x_size, one)

    def drain():
        each(0, 4 * x_size - 1, lambda sender: copy(own, sender, sibling).wait_send())

    Pair.finish = Line.finish = staticmethod(finish)
    Pair.drain = Line.drain = staticmethod(drain)
    return Pair, Line


def each(low, high, step_fn):
    def step(index, carry):
        step_fn(index)
        return carry

    lax.fori_loop(low, high, step, 0)


def kernel(
    planes,
    plane_size,
    head_devices,
    hidden_in,
    self_gain_in,
    cross_gain_in,
    self_query,
    self_key,
    self_value,
    self_out,
    enc_key,
    enc_value,
    cross_query,
    cross_out,
    out,
    hidden,
    self_gain,
    cross_gain,
    weights,
    normed,
    kv,
    qs,
    sent_part,
    sent_level,
    got_part,
    got_level,
    own_part,
    own_level,
    side,
    out_weights,
    last_own,
    last_weights,
    mixed_rows,
    attn_self,
    attn_cross,
    load_sem,
    kv_send,
    kv_recv,
    side_send,
    side_recv,
    so_send,
    so_recv,
    last_send,
    last_recv,
    side_z_send,
    side_z_recv,
    q_send,
    q_recv,
    part_send,
    part_recv,
    level_send,
    level_recv,
    last_z_send,
    last_z_recv,
    so_y_send,
    so_y_recv,
    last_y_send,
    last_y_recv,
    self_send,
    self_recv,
    cross_send,
    cross_recv,
):
    rows, width = hidden.shape
    share = width // head_devices
    x_size = plane_size // 4
    ctx = lax.axis_index("ctx")
    head = lax.axis_index("head")
    plane = ctx // plane_size
    place = ctx % plane_size
    position = (place // 4, (place // 2) % 2, place % 2)
    per_head = planes // head_devices
    last_head = plane // per_head
    last_slot = plane % per_head

    def in_plane(other_place):
        return (plane * plane_size + other_place, head)

    def on_line(other_plane):
        return (other_plane * plane_size + place, head)

    def line_plane(step):
        return (plane + step) % planes

    def head_at(step):
        return (head + step) % head_devices

    def remote(src, dst, send, recv, device):
        return pltpu.make_async_remote_copy(
            src_ref=src,
            dst_ref=dst,
            send_sem=send,
            recv_sem=recv,
            device_id=device,
            device_id_type=MESH,
        )

    barrier = pltpu.get_barrier_semaphore()

    def greet(device):
        pl.semaphore_signal(barrier, inc=1, device_id=device, device_id_type=MESH)

    x, l, core = position

    def line_place(step):
        return lax.rem(x + step, x_size) * 4 + l * 2 + core

    each(1, x_size, lambda step: greet(in_plane(line_place(step))))
    greet(in_plane(x * 4 + (1 - l) * 2 + core))
    greet(in_plane(x * 4 + l * 2 + 1 - core))
    each(1, planes, lambda step: greet(on_line(line_plane(step))))
    each(1, head_devices, lambda step: greet((ctx, head_at(step))))

    loads = [
        pltpu.make_async_copy(source, target, load_sem.at[index])
        for index, (source, target) in enumerate(
            (
                (hidden_in, hidden),
                (self_gain_in, self_gain),
                (self_key, weights.at[0]),
                (self_value, weights.at[1]),
                (self_query, weights.at[2]),
                (self_out, out_weights.at[0]),
                (enc_key, side.at[0, plane, place]),
                (enc_value, side.at[1, plane, place]),
                (cross_query, side.at[2, plane, place]),
                (cross_out, last_own),
                (cross_gain_in, cross_gain),
            )
        )
    ]
    for load in loads:
        load.start()

    loads[0].wait()
    loads[1].wait()
    inputs = hidden[...].astype(jnp.float32)
    mean_square = jnp.mean(inputs * inputs, axis=1, keepdims=True)
    normed[...] = (inputs * lax.rsqrt(mean_square + epsilon) * self_gain[...]).astype(jnp.bfloat16)
    for index in range(2):
        loads[2 + index].wait()
        kv[index, place] = matmul(normed[...], weights[index]).astype(jnp.bfloat16)
    loads[4].wait()
    qs[plane] = matmul(normed[...], weights[2]).astype(jnp.bfloat16)
    for load in loads[5:]:
        load.wait()

    pl.semaphore_wait(barrier, (x_size - 1) + 2 + (planes - 1) + (head_devices - 1))

    sizes = (x_size, plane_size)
    kv_pair, _ = place_gather(
        lambda slot: kv.at[:, slot], kv_send, kv_recv, position, sizes, in_plane
    )
    side_pair, _ = place_gather(
        lambda slot: side.at[:, :, slot], side_send, side_recv, position, sizes, in_plane
    )
    _, so_line = place_gather(
        lambda slot: out_weights.at[pl.ds(1, head_devices - 1), slot],
        so_send,
        so_recv,
        position,
        sizes,
        in_plane,
    )
    last_pair, _ = place_gather(
        lambda slot: last_weights.at[:, :, slot], last_send, last_recv, position, sizes, in_plane
    )

    def query_copy(source_plane, target_plane):
        return remote(
            qs.at[source_plane],
            qs.at[source_plane],
            q_send.at[target_plane],
            q_recv.at[source_plane],
            on_line(target_plane),
        )

    def side_line(step, other):
        block = side.at[:, other, place]
        return remote(
            block, block, side_z_send.at[step], side_z_recv.at[other], on_line(line_plane(step))
        )

    def so_heads(step):
        other = head_at(step)
        return remote(
            out_weights.at[0, place],
            out_weights.at[head_devices - step, place],
            so_y_send.at[step],
            so_y_recv.at[head_devices - step],
            (ctx, other),
        )

    def last_heads(source, target):
        return remote(
            last_own,
            last_weights.at[last_slot, source, place],
            last_y_send.at[0],
            last_y_recv.at[source],
            (ctx, target),
        )

    def last_line(step, slot):
        block = last_weights.at[slot, :, place]
        return remote(
            block, block, last_z_send.at[step], last_z_recv.at[slot], on_line(line_plane(step))
        )

    kv_pair.start()
    kv_pair.start_line()
    each(0, plane, lambda target: query_copy(plane, target).start())
    each(1, head_devices, lambda step: so_heads(step).start())

    @pl.when(head != last_head)
    def _():
        last_heads(head, last_head).start()

    each(1, planes, lambda step: side_line(step, plane).start())
    kv_pair.middle()
    kv_pair.forward()
    kv_pair.forward_across()
    kv_pair.finish()

    each(1, head_devices, lambda step: so_heads(step).wait_recv())
    so_line.start()

    @pl.when(head == last_head)
    def _():
        last_weights[last_slot, head, place] = last_own[...]
        each(1, head_devices, lambda step: last_heads(head_at(step), head).wait_recv())
        each(1, planes, lambda step: last_line(step, last_slot).start())

    each(1, planes, lambda step: side_line(step, line_plane(step)).wait_recv())
    side_pair.start()
    side_pair.start_line()

    key_count = plane_size * rows
    hc = qs.shape[2]

    def part_copy(source_plane, target_plane):
        return remote(
            sent_part.at[target_plane],
            got_part.at[source_plane],
            part_send.at[target_plane],
            part_recv.at[source_plane],
            on_line(target_plane),
        )

    def level_copy(source_plane, target_plane):
        return remote(
            sent_level.at[target_plane],
            got_level.at[source_plane],
            level_send.at[target_plane],
            level_recv.at[source_plane],
            on_line(target_plane),
        )

    each(plane + 1, planes, lambda other: query_copy(other, plane).wait_recv())

    def later_planes(low, high):
        for step in reversed(range(low, high)):
            other = line_plane(step)
            part, levels = attend(
                qs[other], kv[0].reshape(key_count, hc), kv[1].reshape(key_count, hc), None
            )
            sent_part[other] = part.astype(jnp.bfloat16)
            sent_level[other] = to_lanes(levels)

        def send(step):
            part_copy(plane, plane + step).start()
            level_copy(plane, plane + step).start()

        each(low, jnp.minimum(high, planes - plane), send)

    half = planes // 2

    if half > 1:

        @pl.when(plane < half)
        def _():
            later_planes(half, planes)

    part, levels = attend(
        qs[plane], kv[0].reshape(key_count, hc), kv[1].reshape(key_count, hc), place * rows
    )
    own_part[...] = part
    own_level[...] = levels
    later_planes(1, half if half > 1 else planes)

    so_line.forward()
    side_pair.middle()

    def join(other, state):
        mixed, peak, total = state
        part_copy(other, plane).wait_recv()
        level_copy(other, plane).wait_recv()
        level = to_columns(got_level[other], rows)
        new_peak = jnp.maximum(peak, level)
        keep = jnp.exp(peak - new_peak)
        add = jnp.exp(level - new_peak)
        mixed = mixed * spread(keep, hc) + got_part[other].astype(jnp.float32) * spread(add, hc)
        return mixed, new_peak, total * keep + add

    mixed, _, total = lax.fori_loop(
        0, plane, join, (own_part[...], own_level[...], jnp.ones((rows, 128), jnp.float32))
    )
    attn_self[head] = (mixed / spread(total, hc)).astype(jnp.bfloat16)

    def exchange(buffer, send, recv):
        def copy(slot, step):
            return remote(
                buffer.at[slot],
                buffer.at[slot],
                send.at[step],
                recv.at[slot],
                (ctx, head_at(step)),
            )

        def start():
            each(1, head_devices, lambda step: copy(head, step).start())

        def finish(step):
            copy(head_at(step), step).wait_recv()

        def drain():
            each(1, head_devices, lambda step: copy(head, step).wait_send())

        return start, finish, drain

    self_start, self_finish, self_drain = exchange(attn_self, self_send, self_recv)
    self_start()
    so_line.forward_across()
    side_pair.forward()
    so_line.finish()

    def self_term(step):
        return matmul(attn_self[head_at(step)], out_weights[step].reshape(width, hc), NT)

    mixed_rows[...] = hidden[...].astype(jnp.float32) + self_term(0)
    for step in range(1, head_devices):
        self_finish(step)
        mixed_rows[...] += self_term(step)
    whole_rows = mixed_rows[...]
    mean_square = jnp.mean(whole_rows * whole_rows, axis=1, keepdims=True)
    normed[...] = (
        whole_rows * lax.rsqrt(mean_square + epsilon) * cross_gain[...]
    ).astype(jnp.bfloat16)

    def last_arrival(slot):
        @pl.when(plane != head * per_head + slot)
        def _():
            last_line(1, slot).wait_recv()

    each(0, per_head, last_arrival)
    last_pair.start()
    last_pair.start_line()
    side_pair.forward_across()
    side_pair.finish()

    side_rows = planes * plane_size * side.shape[3]
    cross_q = matmul(normed[...], side[2].reshape(side_rows, hc)).astype(jnp.bfloat16)
    crossed, _ = attend(
        cross_q, side[0].reshape(side_rows, hc), side[1].reshape(side_rows, hc), None
    )
    attn_cross[head] = crossed.astype(jnp.bfloat16)
    cross_start, cross_finish, cross_drain = exchange(attn_cross, cross_send, cross_recv)
    cross_start()
    last_pair.middle()
    last_pair.forward()
    last_pair.forward_across()
    last_pair.finish()

    columns = pl.ds(pl.multiple_of(head * share, share), share)
    result = mixed_rows[:, columns]
    for step in range(head_devices):
        if step:
            cross_finish(step)
        other = head_at(step)
        terms = [
            matmul(
                attn_cross[other],
                last_weights[slot, other].reshape(share // per_head, hc),
                NT,
            )
            for slot in range(per_head)
        ]
        result = result + jnp.concatenate(terms, axis=1)
    out[...] = result.astype(jnp.bfloat16)

    each(1, planes, lambda step: side_line(step, plane).wait_send())
    each(1, head_devices, lambda step: so_heads(step).wait_send())

    @pl.when(head != last_head)
    def _():
        last_heads(head, last_head).wait_send()

    @pl.when(head == last_head)
    def _():
        each(1, planes, lambda step: last_line(step, last_slot).wait_send())

    kv_pair.drain()
    side_pair.drain()
    so_line.drain()
    last_pair.drain()
    each(0, plane, lambda target: query_copy(plane, target).wait_send())
    each(plane + 1, planes, lambda other: part_copy(plane, other).wait_send())
    each(plane + 1, planes, lambda other: level_copy(plane, other).wait_send())
    self_drain()
    cross_drain()


def body(
    plane_size,
    hidden,
    self_gain,
    cross_gain,
    self_query,
    self_key,
    self_value,
    self_out,
    cross_query,
    cross_out,
    enc_key,
    enc_value,
):
    rows, width = hidden.shape
    hc = self_query.shape[1]
    ctx_devices = lax.axis_size("ctx")
    head_devices = lax.axis_size("head")
    planes = ctx_devices // plane_size
    share = width // head_devices
    piece = enc_key.shape[0]
    low, full = jnp.bfloat16, jnp.float32
    vmem = pl.BlockSpec(memory_space=pltpu.VMEM)
    hbm = pl.BlockSpec(memory_space=pl.ANY)
    dma = pltpu.SemaphoreType.DMA
    return pl.pallas_call(
        functools.partial(kernel, planes, plane_size, head_devices),
        out_shape=jax.ShapeDtypeStruct((rows, share), low),
        in_specs=[hbm] * 11,
        out_specs=vmem,
        scratch_shapes=[
            pltpu.VMEM((rows, width), low),
            pltpu.VMEM((1, width), full),
            pltpu.VMEM((1, width), full),
            pltpu.VMEM((3, width, hc), low),
            pltpu.VMEM((rows, width), low),
            pltpu.VMEM((2, plane_size, rows, hc), low),
            pltpu.VMEM((planes, rows, hc), low),
            pltpu.VMEM((planes, rows, hc), low),
            pltpu.VMEM((planes, 8, 128), full),
            pltpu.VMEM((planes, rows, hc), low),
            pltpu.VMEM((planes, 8, 128), full),
            pltpu.VMEM((rows, hc), full),
            pltpu.VMEM((rows, 128), full),
            pltpu.VMEM((3, planes, plane_size, piece, hc), low),
            pltpu.VMEM((head_devices, plane_size, width // plane_size, hc), low),
            pltpu.VMEM((piece, hc), low),
            pltpu.VMEM((planes // head_devices, head_devices, plane_size, piece, hc), low),
            pltpu.VMEM((rows, width), full),
            pltpu.VMEM((head_devices, rows, hc), low),
            pltpu.VMEM((head_devices, rows, hc), low),
            dma((11,)),
        ]
        + [dma((plane_size,))] * 8
        + [dma((planes,))] * 10
        + [dma((head_devices,))] * 8,
        compiler_params=pltpu.CompilerParams(
            collective_id=0, has_side_effects=True, vmem_limit_bytes=VMEM_BYTES
        ),
    )(
        hidden,
        self_gain.reshape(1, width),
        cross_gain.reshape(1, width),
        self_query,
        self_key,
        self_value,
        self_out.reshape(plane_size, width // plane_size, hc),
        enc_key,
        enc_value,
        cross_query,
        cross_out,
    )


def solution(mesh, plane_size=PLANE):
    placed = (
        P("ctx", None),
        P(),
        P(),
        P(None, "head"),
        P(None, "head"),
        P(None, "head"),
        P(None, "head"),
        P("ctx", "head"),
        P("ctx", "head"),
        P("ctx", "head"),
        P("ctx", "head"),
    )
    return jax.shard_map(
        functools.partial(body, plane_size),
        mesh=mesh,
        in_specs=placed,
        out_specs=P("ctx", "head"),
        check_vma=False,
    )
```

```python
import functools

import jax
import jax.numpy as jnp
from jax import lax
from jax.experimental import pallas as pl
from jax.experimental.pallas import tpu as pltpu
from jax.sharding import PartitionSpec as P

KV = 64
PLANE = 16
VMEM_BYTES = 62 * 1024 * 1024
MESH = pl.DeviceIdType.MESH

epsilon = 1e-06

NT = (((1,), (1,)), ((), ()))
NN = (((1,), (0,)), ((), ()))


def matmul(left, right, dims=NN):
    return lax.dot_general(left, right, dims, preferred_element_type=jnp.float32)


def to_lanes(columns):
    rows = columns.shape[0]
    square = jnp.concatenate([columns, jnp.zeros((128 - rows, 128), jnp.float32)], axis=0)
    return jnp.transpose(square)[:8]


def to_columns(lanes, rows):
    square = jnp.concatenate([lanes, jnp.zeros((120, 128), jnp.float32)], axis=0)
    return jnp.transpose(square)[:rows]


def spread(per_head, width):
    rows = per_head.shape[0]
    owner = lax.broadcasted_iota(jnp.int32, (rows, width), 1) // KV
    result = jnp.zeros((rows, width), jnp.float32)
    for head in range(width // KV):
        result = jnp.where(owner == head, per_head[:, head : head + 1], result)
    return result


def attend(queries, keys, values, first_query):
    rows, width = queries.shape
    heads = width // KV
    owner = lax.broadcasted_iota(jnp.int32, (rows, width), 1) // KV
    zero = jnp.zeros_like(queries)
    stacked = jnp.concatenate(
        [jnp.where(owner == head, queries, zero) for head in range(heads)], axis=0
    )
    scores = matmul(stacked, keys, NT)
    if first_query is not None:
        token = lax.broadcasted_iota(jnp.int32, (rows, scores.shape[1]), 0) + first_query
        seen = lax.broadcasted_iota(jnp.int32, (rows, scores.shape[1]), 1) <= token
        scores = jnp.where(
            jnp.concatenate([seen] * heads, axis=0), scores, jnp.float32(-1e30)
        )
    peak = jnp.max(scores, axis=1, keepdims=True)
    weights = jnp.exp(scores - peak)
    total = jnp.sum(weights, axis=1, keepdims=True)
    mixed = matmul(weights.astype(jnp.bfloat16), values)
    mixed = mixed / total
    level = peak + jnp.log(total)
    result = jnp.zeros((rows, width), jnp.float32)
    levels = jnp.zeros((rows, 128), jnp.float32)
    column = lax.broadcasted_iota(jnp.int32, (rows, 128), 1)
    for head in range(heads):
        part = slice(head * rows, (head + 1) * rows)
        result = jnp.where(owner == head, mixed[part], result)
        levels = jnp.where(column == head, level[part], levels)
    return result, levels


def place_gather(buffer, send, recv, position, sizes, device_of):
    x, l, core = position
    x_size, device_count = sizes
    own = x * 4 + l * 2 + core
    across = x * 4 + (1 - l) * 2 + core
    sibling = device_of(x * 4 + l * 2 + 1 - core)
    partner = device_of(across)

    def slot_at(step, pair):
        return lax.rem(x + step, x_size) * 4 + pair * 2 + core

    def copy(slot, sender, device):
        return pltpu.make_async_remote_copy(
            src_ref=buffer(slot),
            dst_ref=buffer(slot),
            send_sem=send.at[sender],
            recv_sem=recv.at[slot],
            device_id=device,
            device_id_type=MESH,
        )

    def arrived(slot):
        copy(slot, 0, sibling).wait_recv()

    def to_sibling(slot, sender):
        copy(slot, sender, sibling).start()

    def to_partner(slot, sender):
        copy(slot, sender, partner).start()

    def to_line(slot, sender):
        each(1, x_size, lambda step: copy(slot, sender + step, device_of(slot_at(step, l))).start())

    class Gather:
        @staticmethod
        def start():
            to_partner(own, 0)
            to_sibling(own, 1)

        @staticmethod
        def start_line():
            to_line(own, 1)

        @staticmethod
        def middle():
            arrived(across)
            to_line(across, x_size)
            to_sibling(across, 2 * x_size)

        @staticmethod
        def forward():
            def one(step):
                arrived(slot_at(step, l))
                to_sibling(slot_at(step, l), 2 * x_size + step)

            each(1, x_size, one)

        @staticmethod
        def forward_across():
            def one(step):
                arrived(slot_at(step, 1 - l))
                to_sibling(slot_at(step, 1 - l), 3 * x_size - 1 + step)

            each(1, x_size, one)

        @staticmethod
        def finish():
            each(0, device_count // 2, lambda step: arrived(step * 2 + 1 - core))

        @staticmethod
        def drain():
            each(0, 4 * x_size - 1, lambda sender: copy(own, sender, sibling).wait_send())

    return Gather


def each(low, high, step_fn):
    def step(index, carry):
        step_fn(index)
        return carry

    lax.fori_loop(low, high, step, 0)


def kernel(
    planes,
    plane_size,
    head_devices,
    hidden_in,
    self_gain_in,
    cross_gain_in,
    self_query,
    self_key,
    self_value,
    self_out,
    enc_key,
    enc_value,
    cross_query,
    cross_out,
    out,
    hidden,
    self_gain,
    cross_gain,
    weights,
    normed,
    kv,
    qs,
    sent_part,
    sent_level,
    got_part,
    got_level,
    own_part,
    own_level,
    side,
    out_weights,
    query_own,
    query_weights,
    last_own,
    last_weights,
    mixed_rows,
    gained,
    attn_self,
    attn_cross,
    query_terms,
    got_terms,
    squares,
    load_sem,
    kv_send,
    kv_recv,
    side_send,
    side_recv,
    query_send,
    query_recv,
    last_send,
    last_recv,
    side_z_send,
    side_z_recv,
    q_send,
    q_recv,
    part_send,
    part_recv,
    level_send,
    level_recv,
    query_z_send,
    query_z_recv,
    last_z_send,
    last_z_recv,
    query_y_send,
    query_y_recv,
    last_y_send,
    last_y_recv,
    so_y_send,
    so_y_recv,
    so_c_send,
    so_c_recv,
    self_send,
    self_recv,
    cross_send,
    cross_recv,
    terms_send,
    terms_recv,
    square_send,
    square_recv,
):
    rows, width = hidden.shape
    share = width // head_devices
    x_size = plane_size // 4
    ctx = lax.axis_index("ctx")
    head = lax.axis_index("head")
    plane = ctx // plane_size
    place = ctx % plane_size
    position = (place // 4, (place // 2) % 2, place % 2)
    per_head = planes // head_devices
    columns = pl.ds(pl.multiple_of(head * share, share), share)

    def in_plane(other_place):
        return (plane * plane_size + other_place, head)

    def on_line(other_plane):
        return (other_plane * plane_size + place, head)

    def line_plane(step):
        return (plane + step) % planes

    def head_at(step):
        return (head + step) % head_devices

    def remote(src, dst, send, recv, device):
        return pltpu.make_async_remote_copy(
            src_ref=src,
            dst_ref=dst,
            send_sem=send,
            recv_sem=recv,
            device_id=device,
            device_id_type=MESH,
        )

    barrier = pltpu.get_barrier_semaphore()

    def greet(device):
        pl.semaphore_signal(barrier, inc=1, device_id=device, device_id_type=MESH)

    x, l, core = position

    def line_place(step):
        return lax.rem(x + step, x_size) * 4 + l * 2 + core

    each(1, x_size, lambda step: greet(in_plane(line_place(step))))
    greet(in_plane(x * 4 + (1 - l) * 2 + core))
    greet(in_plane(x * 4 + l * 2 + 1 - core))
    each(1, planes, lambda step: greet(on_line(line_plane(step))))
    each(1, head_devices, lambda step: greet((ctx, head_at(step))))

    loads = [
        pltpu.make_async_copy(source, target, load_sem.at[index])
        for index, (source, target) in enumerate(
            (
                (hidden_in, hidden),
                (self_gain_in, self_gain),
                (self_key, weights.at[0]),
                (self_value, weights.at[1]),
                (self_query, weights.at[2]),
                (self_out.at[head], out_weights.at[head]),
                (enc_key, side.at[0, plane, place]),
                (enc_value, side.at[1, plane, place]),
                (cross_query, query_own),
                (cross_out, last_own),
                (cross_gain_in, cross_gain),
            )
        )
    ]
    for load in loads[:5]:
        load.start()

    loads[0].wait()
    loads[1].wait()
    inputs = hidden[...].astype(jnp.float32)
    mean_square = jnp.mean(inputs * inputs, axis=1, keepdims=True)
    normed[...] = (inputs * lax.rsqrt(mean_square + epsilon) * self_gain[...]).astype(jnp.bfloat16)
    for load in loads[5:]:
        load.start()
    for index in range(2):
        loads[2 + index].wait()
        kv[index, place] = matmul(normed[...], weights[index]).astype(jnp.bfloat16)

    pl.semaphore_wait(barrier, (x_size - 1) + 2 + (planes - 1) + (head_devices - 1))

    sizes = (x_size, plane_size)
    kv_pair = place_gather(
        lambda slot: kv.at[:, slot], kv_send, kv_recv, position, sizes, in_plane
    )
    side_pair = place_gather(
        lambda slot: side.at[:, :, slot], side_send, side_recv, position, sizes, in_plane
    )
    query_pair = place_gather(
        lambda slot: query_weights.at[:, :, slot], query_send, query_recv, position, sizes, in_plane
    )
    last_pair = place_gather(
        lambda slot: last_weights.at[:, :, slot], last_send, last_recv, position, sizes, in_plane
    )

    def query_copy(source_plane, target_plane):
        return remote(
            qs.at[source_plane],
            qs.at[source_plane],
            q_send.at[target_plane],
            q_recv.at[source_plane],
            on_line(target_plane),
        )

    def side_line(step, other):
        block = side.at[:, other, place]
        return remote(
            block, block, side_z_send.at[step], side_z_recv.at[other], on_line(line_plane(step))
        )

    def so_heads(source, target):
        return remote(
            self_out.at[target, core],
            out_weights.at[source, core],
            so_y_send.at[target],
            so_y_recv.at[source],
            (ctx, target),
        )

    def so_sibling(source, half):
        block = out_weights.at[source, half]
        return remote(
            block, block, so_c_send.at[source], so_c_recv.at[source], in_plane(x * 4 + l * 2 + 1 - core)
        )

    def by_features(buffer, own, y_send, y_recv, z_send, z_recv):
        target = plane // per_head
        slot = plane % per_head

        def to_head(source, other):
            return remote(
                own, buffer.at[slot, source, place], y_send.at[0], y_recv.at[source], (ctx, other)
            )

        def line(step, which):
            block = buffer.at[which, :, place]
            return remote(block, block, z_send.at[step], z_recv.at[which], on_line(line_plane(step)))

        def start():
            @pl.when(head != target)
            def _():
                to_head(head, target).start()

        def start_line():
            @pl.when(head == target)
            def _():
                buffer[slot, head, place] = own[...]
                each(1, head_devices, lambda step: to_head(head_at(step), head).wait_recv())
                each(1, planes, lambda step: line(step, slot).start())

        def finish():
            def arrival(which):
                @pl.when(plane != head * per_head + which)
                def _():
                    line(1, which).wait_recv()

            each(0, per_head, arrival)

        def drain():
            @pl.when(head != target)
            def _():
                to_head(head, target).wait_send()

            @pl.when(head == target)
            def _():
                each(1, planes, lambda step: line(step, slot).wait_send())

        return start, start_line, finish, drain

    query_start, query_line, query_finish, query_drain = by_features(
        query_weights, query_own, query_y_send, query_y_recv, query_z_send, query_z_recv
    )
    last_start, last_line, last_finish, last_drain = by_features(
        last_weights, last_own, last_y_send, last_y_recv, last_z_send, last_z_recv
    )

    kv_pair.start()
    kv_pair.start_line()
    loads[4].wait()
    qs[plane] = matmul(normed[...], weights[2]).astype(jnp.bfloat16)
    each(0, plane, lambda target: query_copy(plane, target).start())
    for load in loads[5:]:
        load.wait()
    query_start()
    last_start()
    each(1, head_devices, lambda step: so_heads(head, head_at(step)).start())
    each(1, planes, lambda step: side_line(step, plane).start())
    kv_pair.middle()
    query_line()
    last_line()
    kv_pair.forward()
    kv_pair.forward_across()
    kv_pair.finish()

    each(1, planes, lambda step: side_line(step, line_plane(step)).wait_recv())
    side_pair.start()
    side_pair.start_line()

    key_count = plane_size * rows
    hc = qs.shape[2]

    def part_copy(source_plane, target_plane):
        return remote(
            sent_part.at[target_plane],
            got_part.at[source_plane],
            part_send.at[target_plane],
            part_recv.at[source_plane],
            on_line(target_plane),
        )

    def level_copy(source_plane, target_plane):
        return remote(
            sent_level.at[target_plane],
            got_level.at[source_plane],
            level_send.at[target_plane],
            level_recv.at[source_plane],
            on_line(target_plane),
        )

    each(plane + 1, planes, lambda other: query_copy(other, plane).wait_recv())

    def later_planes(low, high):
        for step in reversed(range(low, high)):
            other = line_plane(step)
            part, levels = attend(
                qs[other], kv[0].reshape(key_count, hc), kv[1].reshape(key_count, hc), None
            )
            sent_part[other] = part.astype(jnp.bfloat16)
            sent_level[other] = to_lanes(levels)

        def send(step):
            part_copy(plane, plane + step).start()
            level_copy(plane, plane + step).start()

        each(low, jnp.minimum(high, planes - plane), send)

    half = planes // 2

    if half > 1:

        @pl.when(plane < half)
        def _():
            later_planes(half, planes)

    query_finish()
    query_pair.start()
    query_pair.start_line()

    later_planes(1, half if half > 1 else planes)
    part, levels = attend(
        qs[plane], kv[0].reshape(key_count, hc), kv[1].reshape(key_count, hc), place * rows
    )
    own_part[...] = part
    own_level[...] = levels

    query_pair.middle()
    side_pair.middle()
    last_finish()
    last_pair.start()
    last_pair.start_line()

    def so_arrival(step):
        other = head_at(step)
        so_heads(other, head).wait_recv()
        so_sibling(other, core).start()

    each(1, head_devices, so_arrival)

    def join(other, state):
        mixed, peak, total = state
        part_copy(other, plane).wait_recv()
        level_copy(other, plane).wait_recv()
        level = to_columns(got_level[other], rows)
        new_peak = jnp.maximum(peak, level)
        keep = jnp.exp(peak - new_peak)
        add = jnp.exp(level - new_peak)
        mixed = mixed * spread(keep, hc) + got_part[other].astype(jnp.float32) * spread(add, hc)
        return mixed, new_peak, total * keep + add

    mixed, _, total = lax.fori_loop(
        0, plane, join, (own_part[...], own_level[...], jnp.ones((rows, 128), jnp.float32))
    )
    attn_self[head] = (mixed / spread(total, hc)).astype(jnp.bfloat16)

    def exchange(buffer, send, recv):
        def copy(slot, step):
            return remote(
                buffer.at[slot],
                buffer.at[slot],
                send.at[step],
                recv.at[slot],
                (ctx, head_at(step)),
            )

        def start():
            each(1, head_devices, lambda step: copy(head, step).start())

        def finish(step):
            copy(head_at(step), step).wait_recv()

        def drain():
            each(1, head_devices, lambda step: copy(head, step).wait_send())

        return start, finish, drain

    self_start, self_finish, self_drain = exchange(attn_self, self_send, self_recv)
    self_start()
    last_pair.middle()
    query_pair.forward()
    side_pair.forward()
    each(1, head_devices, lambda step: so_sibling(head_at(step), 1 - core).wait_recv())

    def self_term(step):
        other = head_at(step)
        return matmul(attn_self[other], out_weights[other].reshape(share, hc), NT)

    mixed = hidden[:, columns].astype(jnp.float32) + self_term(0)
    for step in range(1, head_devices):
        self_finish(step)
        mixed = mixed + self_term(step)
    mixed_rows[...] = mixed

    square = jnp.sum(mixed * mixed, axis=1, keepdims=True)
    squares[head] = to_lanes(jnp.broadcast_to(square, (rows, 128)))
    square_start, square_finish, square_drain = exchange(squares, square_send, square_recv)
    square_start()
    gained[...] = (mixed * cross_gain[:, columns]).astype(jnp.bfloat16)
    query_pair.forward_across()
    query_pair.finish()
    piece_rows = share // per_head

    def query_term(other):
        return sum(
            matmul(
                gained[:, slot * piece_rows : (slot + 1) * piece_rows],
                query_weights[slot, other].reshape(piece_rows, hc),
            )
            for slot in range(per_head)
        )

    def term_copy(step, slot):
        other = head_at(step)
        return remote(
            query_terms.at[other],
            got_terms.at[slot],
            terms_send.at[step],
            terms_recv.at[slot],
            (ctx, other),
        )

    for step in range(1, head_devices):
        query_terms[head_at(step)] = query_term(head_at(step)).astype(jnp.bfloat16)
        term_copy(step, head).start()
    cross_q = query_term(head)

    side_pair.forward_across()
    last_pair.forward()
    side_pair.finish()
    all_squares = squares[head]
    for step in range(1, head_devices):
        square_finish(step)
        all_squares = all_squares + squares[head_at(step)]
        term_copy(step, head_at(step)).wait_recv()
        cross_q = cross_q + got_terms[head_at(step)].astype(jnp.float32)
    scale = lax.rsqrt(to_columns(all_squares, rows)[:, :1] / width + epsilon)
    cross_q = (cross_q * scale).astype(jnp.bfloat16)

    side_rows = planes * plane_size * side.shape[3]
    crossed, _ = attend(
        cross_q, side[0].reshape(side_rows, hc), side[1].reshape(side_rows, hc), None
    )
    attn_cross[head] = crossed.astype(jnp.bfloat16)
    cross_start, cross_finish, cross_drain = exchange(attn_cross, cross_send, cross_recv)
    cross_start()
    last_pair.forward_across()
    last_pair.finish()

    result = mixed_rows[...]
    for step in range(head_devices):
        if step:
            cross_finish(step)
        other = head_at(step)
        terms = [
            matmul(
                attn_cross[other],
                last_weights[slot, other].reshape(share // per_head, hc),
                NT,
            )
            for slot in range(per_head)
        ]
        result = result + jnp.concatenate(terms, axis=1)
    out[...] = result.astype(jnp.bfloat16)

    each(1, planes, lambda step: side_line(step, plane).wait_send())
    each(1, head_devices, lambda step: so_heads(head, head_at(step)).wait_send())
    each(1, head_devices, lambda step: so_sibling(head_at(step), core).wait_send())
    query_drain()
    last_drain()
    kv_pair.drain()
    side_pair.drain()
    query_pair.drain()
    last_pair.drain()
    each(0, plane, lambda target: query_copy(plane, target).wait_send())
    each(plane + 1, planes, lambda other: part_copy(plane, other).wait_send())
    each(plane + 1, planes, lambda other: level_copy(plane, other).wait_send())
    self_drain()
    cross_drain()
    square_drain()
    each(1, head_devices, lambda step: term_copy(step, head).wait_send())


def body(
    plane_size,
    hidden,
    self_gain,
    cross_gain,
    self_query,
    self_key,
    self_value,
    self_out,
    cross_query,
    cross_out,
    enc_key,
    enc_value,
):
    rows, width = hidden.shape
    hc = self_query.shape[1]
    ctx_devices = lax.axis_size("ctx")
    head_devices = lax.axis_size("head")
    planes = ctx_devices // plane_size
    share = width // head_devices
    piece = enc_key.shape[0]
    low, full = jnp.bfloat16, jnp.float32
    vmem = pl.BlockSpec(memory_space=pltpu.VMEM)
    hbm = pl.BlockSpec(memory_space=pl.ANY)
    dma = pltpu.SemaphoreType.DMA
    return pl.pallas_call(
        functools.partial(kernel, planes, plane_size, head_devices),
        out_shape=jax.ShapeDtypeStruct((rows, share), low),
        in_specs=[hbm] * 11,
        out_specs=vmem,
        scratch_shapes=[
            pltpu.VMEM((rows, width), low),
            pltpu.VMEM((1, width), full),
            pltpu.VMEM((1, width), full),
            pltpu.VMEM((3, width, hc), low),
            pltpu.VMEM((rows, width), low),
            pltpu.VMEM((2, plane_size, rows, hc), low),
            pltpu.VMEM((planes, rows, hc), low),
            pltpu.VMEM((planes, rows, hc), low),
            pltpu.VMEM((planes, 8, 128), full),
            pltpu.VMEM((planes, rows, hc), low),
            pltpu.VMEM((planes, 8, 128), full),
            pltpu.VMEM((rows, hc), full),
            pltpu.VMEM((rows, 128), full),
            pltpu.VMEM((2, planes, plane_size, piece, hc), low),
            pltpu.VMEM((head_devices, 2, share // 2, hc), low),
            pltpu.VMEM((piece, hc), low),
            pltpu.VMEM((planes // head_devices, head_devices, plane_size, piece, hc), low),
            pltpu.VMEM((piece, hc), low),
            pltpu.VMEM((planes // head_devices, head_devices, plane_size, piece, hc), low),
            pltpu.VMEM((rows, share), full),
            pltpu.VMEM((rows, share), low),
            pltpu.VMEM((head_devices, rows, hc), low),
            pltpu.VMEM((head_devices, rows, hc), low),
            pltpu.VMEM((head_devices, rows, hc), low),
            pltpu.VMEM((head_devices, rows, hc), low),
            pltpu.VMEM((head_devices, 8, 128), full),
            dma((11,)),
        ]
        + [dma((plane_size,))] * 8
        + [dma((planes,))] * 12
        + [dma((head_devices,))] * 16,
        compiler_params=pltpu.CompilerParams(
            collective_id=0, has_side_effects=True, vmem_limit_bytes=VMEM_BYTES
        ),
    )(
        hidden,
        self_gain.reshape(1, width),
        cross_gain.reshape(1, width),
        self_query,
        self_key,
        self_value,
        self_out.reshape(head_devices, 2, share // 2, hc),
        enc_key,
        enc_value,
        cross_query,
        cross_out,
    )


def solution(mesh, plane_size=PLANE):
    placed = (
        P("ctx", None),
        P(),
        P(),
        P(None, "head"),
        P(None, "head"),
        P(None, "head"),
        P(None, "head"),
        P("ctx", "head"),
        P("ctx", "head"),
        P("ctx", "head"),
        P("ctx", "head"),
    )
    return jax.shard_map(
        functools.partial(body, plane_size),
        mesh=mesh,
        in_specs=placed,
        out_specs=P("ctx", "head"),
        check_vma=False,
    )
```

```python
import functools

import jax
import jax.numpy as jnp
from jax import lax
from jax.experimental import pallas as pl
from jax.experimental.pallas import tpu as pltpu
from jax.sharding import PartitionSpec as P

KV = 64
PLANE = 16
VMEM_BYTES = 62 * 1024 * 1024
MESH = pl.DeviceIdType.MESH

epsilon = 1e-06

NT = (((1,), (1,)), ((), ()))
NN = (((1,), (0,)), ((), ()))


def matmul(left, right, dims=NN):
    return lax.dot_general(left, right, dims, preferred_element_type=jnp.float32)


def to_lanes(columns):
    rows = columns.shape[0]
    square = jnp.concatenate([columns, jnp.zeros((128 - rows, 128), jnp.float32)], axis=0)
    return jnp.transpose(square)[:8]


def to_columns(lanes, rows):
    square = jnp.concatenate([lanes, jnp.zeros((120, 128), jnp.float32)], axis=0)
    return jnp.transpose(square)[:rows]


def spread(per_head, width):
    rows = per_head.shape[0]
    owner = lax.broadcasted_iota(jnp.int32, (rows, width), 1) // KV
    result = jnp.zeros((rows, width), jnp.float32)
    for head in range(width // KV):
        result = jnp.where(owner == head, per_head[:, head : head + 1], result)
    return result


def attend(queries, keys, values, first_query):
    rows, width = queries.shape
    heads = width // KV
    owner = lax.broadcasted_iota(jnp.int32, (rows, width), 1) // KV
    zero = jnp.zeros_like(queries)
    stacked = jnp.concatenate(
        [jnp.where(owner == head, queries, zero) for head in range(heads)], axis=0
    )
    scores = matmul(stacked, keys, NT)
    if first_query is not None:
        token = lax.broadcasted_iota(jnp.int32, (rows, scores.shape[1]), 0) + first_query
        seen = lax.broadcasted_iota(jnp.int32, (rows, scores.shape[1]), 1) <= token
        scores = jnp.where(
            jnp.concatenate([seen] * heads, axis=0), scores, jnp.float32(-1e30)
        )
    peak = jnp.max(scores, axis=1, keepdims=True)
    weights = jnp.exp(scores - peak)
    total = jnp.sum(weights, axis=1, keepdims=True)
    mixed = matmul(weights.astype(jnp.bfloat16), values)
    mixed = mixed / total
    level = peak + jnp.log(total)
    result = jnp.zeros((rows, width), jnp.float32)
    levels = jnp.zeros((rows, 128), jnp.float32)
    column = lax.broadcasted_iota(jnp.int32, (rows, 128), 1)
    for head in range(heads):
        part = slice(head * rows, (head + 1) * rows)
        result = jnp.where(owner == head, mixed[part], result)
        levels = jnp.where(column == head, level[part], levels)
    return result, levels


def place_gather(buffer, send, recv, position, sizes, device_of):
    x, l, core = position
    x_size, device_count = sizes
    own = x * 4 + l * 2 + core
    across = x * 4 + (1 - l) * 2 + core
    sibling = device_of(x * 4 + l * 2 + 1 - core)
    partner = device_of(across)

    def slot_at(step, pair):
        return lax.rem(x + step, x_size) * 4 + pair * 2 + core

    def copy(slot, sender, device):
        return pltpu.make_async_remote_copy(
            src_ref=buffer(slot),
            dst_ref=buffer(slot),
            send_sem=send.at[sender],
            recv_sem=recv.at[slot],
            device_id=device,
            device_id_type=MESH,
        )

    def arrived(slot):
        copy(slot, 0, sibling).wait_recv()

    def to_sibling(slot, sender):
        copy(slot, sender, sibling).start()

    def to_partner(slot, sender):
        copy(slot, sender, partner).start()

    def to_line(slot, sender):
        each(1, x_size, lambda step: copy(slot, sender + step, device_of(slot_at(step, l))).start())

    class Gather:
        @staticmethod
        def start():
            to_partner(own, 0)
            to_sibling(own, 1)

        @staticmethod
        def start_line():
            to_line(own, 1)

        @staticmethod
        def middle():
            arrived(across)
            to_line(across, x_size)
            to_sibling(across, 2 * x_size)

        @staticmethod
        def forward():
            def one(step):
                arrived(slot_at(step, l))
                to_sibling(slot_at(step, l), 2 * x_size + step)

            each(1, x_size, one)

        @staticmethod
        def forward_across():
            def one(step):
                arrived(slot_at(step, 1 - l))
                to_sibling(slot_at(step, 1 - l), 3 * x_size - 1 + step)

            each(1, x_size, one)

        @staticmethod
        def finish():
            each(0, device_count // 2, lambda step: arrived(step * 2 + 1 - core))

        @staticmethod
        def drain():
            each(0, 4 * x_size - 1, lambda sender: copy(own, sender, sibling).wait_send())

    return Gather


def each(low, high, step_fn):
    def step(index, carry):
        step_fn(index)
        return carry

    lax.fori_loop(low, high, step, 0)


def kernel(
    planes,
    plane_size,
    head_devices,
    hidden_in,
    self_gain_in,
    cross_gain_in,
    self_query,
    self_key,
    self_value,
    self_out,
    enc_key,
    enc_value,
    cross_query,
    cross_out,
    out,
    hidden,
    self_gain,
    cross_gain,
    weights,
    normed,
    kv,
    qs,
    sent_part,
    sent_level,
    got_part,
    got_level,
    own_part,
    own_level,
    side,
    out_weights,
    query_own,
    query_weights,
    last_own,
    last_weights,
    mixed_rows,
    gained,
    attn_self,
    attn_cross,
    query_terms,
    got_terms,
    squares,
    load_sem,
    kv_send,
    kv_recv,
    side_send,
    side_recv,
    query_send,
    query_recv,
    last_send,
    last_recv,
    side_z_send,
    side_z_recv,
    q_send,
    q_recv,
    part_send,
    part_recv,
    level_send,
    level_recv,
    query_z_send,
    query_z_recv,
    last_z_send,
    last_z_recv,
    query_y_send,
    query_y_recv,
    last_y_send,
    last_y_recv,
    so_y_send,
    so_y_recv,
    so_c_send,
    so_c_recv,
    self_send,
    self_recv,
    cross_send,
    cross_recv,
    terms_send,
    terms_recv,
    square_send,
    square_recv,
):
    rows, width = hidden.shape
    share = width // head_devices
    x_size = plane_size // 4
    ctx = lax.axis_index("ctx")
    head = lax.axis_index("head")
    plane = ctx // plane_size
    place = ctx % plane_size
    position = (place // 4, (place // 2) % 2, place % 2)
    per_head = planes // head_devices
    columns = pl.ds(pl.multiple_of(head * share, share), share)

    def in_plane(other_place):
        return (plane * plane_size + other_place, head)

    def on_line(other_plane):
        return (other_plane * plane_size + place, head)

    def line_plane(step):
        return (plane + step) % planes

    def head_at(step):
        return (head + step) % head_devices

    def remote(src, dst, send, recv, device):
        return pltpu.make_async_remote_copy(
            src_ref=src,
            dst_ref=dst,
            send_sem=send,
            recv_sem=recv,
            device_id=device,
            device_id_type=MESH,
        )

    barrier = pltpu.get_barrier_semaphore()

    def greet(device):
        pl.semaphore_signal(barrier, inc=1, device_id=device, device_id_type=MESH)

    x, l, core = position

    def line_place(step):
        return lax.rem(x + step, x_size) * 4 + l * 2 + core

    each(1, x_size, lambda step: greet(in_plane(line_place(step))))
    greet(in_plane(x * 4 + (1 - l) * 2 + core))
    greet(in_plane(x * 4 + l * 2 + 1 - core))
    each(1, planes, lambda step: greet(on_line(line_plane(step))))
    each(1, head_devices, lambda step: greet((ctx, head_at(step))))

    loads = [
        pltpu.make_async_copy(source, target, load_sem.at[index])
        for index, (source, target) in enumerate(
            (
                (hidden_in, hidden),
                (self_gain_in, self_gain),
                (self_key, weights.at[0]),
                (self_value, weights.at[1]),
                (self_query, weights.at[2]),
                (self_out.at[head], out_weights.at[head]),
                (enc_key, side.at[0, plane, place]),
                (enc_value, side.at[1, plane, place]),
                (cross_query, query_own),
                (cross_out, last_own),
                (cross_gain_in, cross_gain),
            )
        )
    ]
    for load in loads[:5]:
        load.start()

    loads[0].wait()
    loads[1].wait()
    inputs = hidden[...].astype(jnp.float32)
    mean_square = jnp.mean(inputs * inputs, axis=1, keepdims=True)
    normed[...] = (inputs * lax.rsqrt(mean_square + epsilon) * self_gain[...]).astype(jnp.bfloat16)
    for load in loads[5:]:
        load.start()
    for index in range(2):
        loads[2 + index].wait()
        kv[index, place] = matmul(normed[...], weights[index]).astype(jnp.bfloat16)

    pl.semaphore_wait(barrier, (x_size - 1) + 2 + (planes - 1) + (head_devices - 1))

    sizes = (x_size, plane_size)
    kv_pair = place_gather(
        lambda slot: kv.at[:, slot], kv_send, kv_recv, position, sizes, in_plane
    )
    side_pair = place_gather(
        lambda slot: side.at[:, :, slot], side_send, side_recv, position, sizes, in_plane
    )
    query_pair = place_gather(
        lambda slot: query_weights.at[:, :, slot], query_send, query_recv, position, sizes, in_plane
    )
    last_pair = place_gather(
        lambda slot: last_weights.at[:, :, slot], last_send, last_recv, position, sizes, in_plane
    )

    def query_copy(source_plane, target_plane):
        return remote(
            qs.at[source_plane],
            qs.at[source_plane],
            q_send.at[target_plane],
            q_recv.at[source_plane],
            on_line(target_plane),
        )

    def side_line(step, other):
        block = side.at[:, other, place]
        return remote(
            block, block, side_z_send.at[step], side_z_recv.at[other], on_line(line_plane(step))
        )

    def so_heads(source, target):
        return remote(
            self_out.at[target, core],
            out_weights.at[source, core],
            so_y_send.at[target],
            so_y_recv.at[source],
            (ctx, target),
        )

    def so_sibling(source, half):
        block = out_weights.at[source, half]
        return remote(
            block, block, so_c_send.at[source], so_c_recv.at[source], in_plane(x * 4 + l * 2 + 1 - core)
        )

    def by_features(buffer, own, y_send, y_recv, z_send, z_recv):
        target = plane // per_head
        slot = plane % per_head

        def to_head(source, other):
            return remote(
                own, buffer.at[slot, source, place], y_send.at[0], y_recv.at[source], (ctx, other)
            )

        def line(step, which):
            block = buffer.at[which, :, place]
            return remote(block, block, z_send.at[step], z_recv.at[which], on_line(line_plane(step)))

        def start():
            @pl.when(head != target)
            def _():
                to_head(head, target).start()

        def start_line():
            @pl.when(head == target)
            def _():
                buffer[slot, head, place] = own[...]
                each(1, head_devices, lambda step: to_head(head_at(step), head).wait_recv())
                each(1, planes, lambda step: line(step, slot).start())

        def finish():
            def arrival(which):
                @pl.when(plane != head * per_head + which)
                def _():
                    line(1, which).wait_recv()

            each(0, per_head, arrival)

        def drain():
            @pl.when(head != target)
            def _():
                to_head(head, target).wait_send()

            @pl.when(head == target)
            def _():
                each(1, planes, lambda step: line(step, slot).wait_send())

        return start, start_line, finish, drain

    query_start, query_line, query_finish, query_drain = by_features(
        query_weights, query_own, query_y_send, query_y_recv, query_z_send, query_z_recv
    )
    last_start, last_line, last_finish, last_drain = by_features(
        last_weights, last_own, last_y_send, last_y_recv, last_z_send, last_z_recv
    )

    kv_pair.start()
    kv_pair.start_line()
    for load in loads[5:]:
        load.wait()
    query_start()
    last_start()
    each(1, planes, lambda step: side_line(step, plane).start())
    loads[4].wait()
    qs[plane] = matmul(normed[...], weights[2]).astype(jnp.bfloat16)
    each(0, plane, lambda target: query_copy(plane, target).start())
    each(1, head_devices, lambda step: so_heads(head, head_at(step)).start())
    kv_pair.middle()
    query_line()
    last_line()
    kv_pair.forward()
    kv_pair.forward_across()
    kv_pair.finish()

    each(1, planes, lambda step: side_line(step, line_plane(step)).wait_recv())
    side_pair.start()
    side_pair.start_line()

    key_count = plane_size * rows
    hc = qs.shape[2]

    def part_copy(source_plane, target_plane):
        return remote(
            sent_part.at[target_plane],
            got_part.at[source_plane],
            part_send.at[target_plane],
            part_recv.at[source_plane],
            on_line(target_plane),
        )

    def level_copy(source_plane, target_plane):
        return remote(
            sent_level.at[target_plane],
            got_level.at[source_plane],
            level_send.at[target_plane],
            level_recv.at[source_plane],
            on_line(target_plane),
        )

    each(plane + 1, planes, lambda other: query_copy(other, plane).wait_recv())

    def later_planes(low, high):
        for step in reversed(range(low, high)):
            other = line_plane(step)
            part, levels = attend(
                qs[other], kv[0].reshape(key_count, hc), kv[1].reshape(key_count, hc), None
            )
            sent_part[other] = part.astype(jnp.bfloat16)
            sent_level[other] = to_lanes(levels)

        def send(step):
            part_copy(plane, plane + step).start()
            level_copy(plane, plane + step).start()

        each(low, jnp.minimum(high, planes - plane), send)

    half = planes // 2

    if half > 1:

        @pl.when(plane < half)
        def _():
            later_planes(half, planes)

    query_finish()
    query_pair.start()
    query_pair.start_line()

    later_planes(1, half if half > 1 else planes)
    part, levels = attend(
        qs[plane], kv[0].reshape(key_count, hc), kv[1].reshape(key_count, hc), place * rows
    )
    own_part[...] = part
    own_level[...] = levels

    query_pair.middle()
    side_pair.middle()
    last_finish()
    last_pair.start()
    last_pair.start_line()

    def so_arrival(step):
        other = head_at(step)
        so_heads(other, head).wait_recv()
        so_sibling(other, core).start()

    each(1, head_devices, so_arrival)

    def join(other, state):
        mixed, peak, total = state
        part_copy(other, plane).wait_recv()
        level_copy(other, plane).wait_recv()
        level = to_columns(got_level[other], rows)
        new_peak = jnp.maximum(peak, level)
        keep = jnp.exp(peak - new_peak)
        add = jnp.exp(level - new_peak)
        mixed = mixed * spread(keep, hc) + got_part[other].astype(jnp.float32) * spread(add, hc)
        return mixed, new_peak, total * keep + add

    mixed, _, total = lax.fori_loop(
        0, plane, join, (own_part[...], own_level[...], jnp.ones((rows, 128), jnp.float32))
    )
    attn_self[head] = (mixed / spread(total, hc)).astype(jnp.bfloat16)

    def exchange(buffer, send, recv):
        def copy(slot, step):
            return remote(
                buffer.at[slot],
                buffer.at[slot],
                send.at[step],
                recv.at[slot],
                (ctx, head_at(step)),
            )

        def start():
            each(1, head_devices, lambda step: copy(head, step).start())

        def finish(step):
            copy(head_at(step), step).wait_recv()

        def drain():
            each(1, head_devices, lambda step: copy(head, step).wait_send())

        return start, finish, drain

    self_start, self_finish, self_drain = exchange(attn_self, self_send, self_recv)
    self_start()
    last_pair.middle()
    query_pair.forward()
    side_pair.forward()
    each(1, head_devices, lambda step: so_sibling(head_at(step), 1 - core).wait_recv())

    def self_term(step):
        other = head_at(step)
        return matmul(attn_self[other], out_weights[other].reshape(share, hc), NT)

    mixed = hidden[:, columns].astype(jnp.float32) + self_term(0)
    for step in range(1, head_devices):
        self_finish(step)
        mixed = mixed + self_term(step)
    mixed_rows[...] = mixed

    square = jnp.sum(mixed * mixed, axis=1, keepdims=True)
    squares[head] = to_lanes(jnp.broadcast_to(square, (rows, 128)))
    square_start, square_finish, square_drain = exchange(squares, square_send, square_recv)
    square_start()
    gained[...] = (mixed * cross_gain[:, columns]).astype(jnp.bfloat16)
    query_pair.forward_across()
    query_pair.finish()
    piece_rows = share // per_head

    def query_term(other):
        return sum(
            matmul(
                gained[:, slot * piece_rows : (slot + 1) * piece_rows],
                query_weights[slot, other].reshape(piece_rows, hc),
            )
            for slot in range(per_head)
        )

    def term_copy(step, slot):
        other = head_at(step)
        return remote(
            query_terms.at[other],
            got_terms.at[slot],
            terms_send.at[step],
            terms_recv.at[slot],
            (ctx, other),
        )

    for step in range(1, head_devices):
        query_terms[head_at(step)] = query_term(head_at(step)).astype(jnp.bfloat16)
        term_copy(step, head).start()
    cross_q = query_term(head)

    side_pair.forward_across()
    last_pair.forward()
    side_pair.finish()
    all_squares = squares[head]
    for step in range(1, head_devices):
        square_finish(step)
        all_squares = all_squares + squares[head_at(step)]
        term_copy(step, head_at(step)).wait_recv()
        cross_q = cross_q + got_terms[head_at(step)].astype(jnp.float32)
    scale = lax.rsqrt(to_columns(all_squares, rows)[:, :1] / width + epsilon)
    cross_q = (cross_q * scale).astype(jnp.bfloat16)

    side_rows = planes * plane_size * side.shape[3]
    crossed, _ = attend(
        cross_q, side[0].reshape(side_rows, hc), side[1].reshape(side_rows, hc), None
    )
    attn_cross[head] = crossed.astype(jnp.bfloat16)
    cross_start, cross_finish, cross_drain = exchange(attn_cross, cross_send, cross_recv)
    cross_start()
    last_pair.forward_across()
    last_pair.finish()

    result = mixed_rows[...]
    for step in range(head_devices):
        if step:
            cross_finish(step)
        other = head_at(step)
        terms = [
            matmul(
                attn_cross[other],
                last_weights[slot, other].reshape(share // per_head, hc),
                NT,
            )
            for slot in range(per_head)
        ]
        result = result + jnp.concatenate(terms, axis=1)
    out[...] = result.astype(jnp.bfloat16)

    each(1, planes, lambda step: side_line(step, plane).wait_send())
    each(1, head_devices, lambda step: so_heads(head, head_at(step)).wait_send())
    each(1, head_devices, lambda step: so_sibling(head_at(step), core).wait_send())
    query_drain()
    last_drain()
    kv_pair.drain()
    side_pair.drain()
    query_pair.drain()
    last_pair.drain()
    each(0, plane, lambda target: query_copy(plane, target).wait_send())
    each(plane + 1, planes, lambda other: part_copy(plane, other).wait_send())
    each(plane + 1, planes, lambda other: level_copy(plane, other).wait_send())
    self_drain()
    cross_drain()
    square_drain()
    each(1, head_devices, lambda step: term_copy(step, head).wait_send())


def body(
    plane_size,
    hidden,
    self_gain,
    cross_gain,
    self_query,
    self_key,
    self_value,
    self_out,
    cross_query,
    cross_out,
    enc_key,
    enc_value,
):
    rows, width = hidden.shape
    hc = self_query.shape[1]
    ctx_devices = lax.axis_size("ctx")
    head_devices = lax.axis_size("head")
    planes = ctx_devices // plane_size
    share = width // head_devices
    piece = enc_key.shape[0]
    low, full = jnp.bfloat16, jnp.float32
    vmem = pl.BlockSpec(memory_space=pltpu.VMEM)
    hbm = pl.BlockSpec(memory_space=pl.ANY)
    dma = pltpu.SemaphoreType.DMA
    return pl.pallas_call(
        functools.partial(kernel, planes, plane_size, head_devices),
        out_shape=jax.ShapeDtypeStruct((rows, share), low),
        in_specs=[hbm] * 11,
        out_specs=vmem,
        scratch_shapes=[
            pltpu.VMEM((rows, width), low),
            pltpu.VMEM((1, width), full),
            pltpu.VMEM((1, width), full),
            pltpu.VMEM((3, width, hc), low),
            pltpu.VMEM((rows, width), low),
            pltpu.VMEM((2, plane_size, rows, hc), low),
            pltpu.VMEM((planes, rows, hc), low),
            pltpu.VMEM((planes, rows, hc), low),
            pltpu.VMEM((planes, 8, 128), full),
            pltpu.VMEM((planes, rows, hc), low),
            pltpu.VMEM((planes, 8, 128), full),
            pltpu.VMEM((rows, hc), full),
            pltpu.VMEM((rows, 128), full),
            pltpu.VMEM((2, planes, plane_size, piece, hc), low),
            pltpu.VMEM((head_devices, 2, share // 2, hc), low),
            pltpu.VMEM((piece, hc), low),
            pltpu.VMEM((planes // head_devices, head_devices, plane_size, piece, hc), low),
            pltpu.VMEM((piece, hc), low),
            pltpu.VMEM((planes // head_devices, head_devices, plane_size, piece, hc), low),
            pltpu.VMEM((rows, share), full),
            pltpu.VMEM((rows, share), low),
            pltpu.VMEM((head_devices, rows, hc), low),
            pltpu.VMEM((head_devices, rows, hc), low),
            pltpu.VMEM((head_devices, rows, hc), low),
            pltpu.VMEM((head_devices, rows, hc), low),
            pltpu.VMEM((head_devices, 8, 128), full),
            dma((11,)),
        ]
        + [dma((plane_size,))] * 8
        + [dma((planes,))] * 12
        + [dma((head_devices,))] * 16,
        compiler_params=pltpu.CompilerParams(
            collective_id=0, has_side_effects=True, vmem_limit_bytes=VMEM_BYTES
        ),
    )(
        hidden,
        self_gain.reshape(1, width),
        cross_gain.reshape(1, width),
        self_query,
        self_key,
        self_value,
        self_out.reshape(head_devices, 2, share // 2, hc),
        enc_key,
        enc_value,
        cross_query,
        cross_out,
    )


def solution(mesh, plane_size=PLANE):
    placed = (
        P("ctx", None),
        P(),
        P(),
        P(None, "head"),
        P(None, "head"),
        P(None, "head"),
        P(None, "head"),
        P("ctx", "head"),
        P("ctx", "head"),
        P("ctx", "head"),
        P("ctx", "head"),
    )
    return jax.shard_map(
        functools.partial(body, plane_size),
        mesh=mesh,
        in_specs=placed,
        out_specs=P("ctx", "head"),
        check_vma=False,
    )
```

```python
import functools

import jax
import jax.numpy as jnp
from jax import lax
from jax.experimental import pallas as pl
from jax.experimental.pallas import tpu as pltpu
from jax.sharding import PartitionSpec as P

KV = 64
PLANE = 16
VMEM_BYTES = 62 * 1024 * 1024
MESH = pl.DeviceIdType.MESH

epsilon = 1e-06

NT = (((1,), (1,)), ((), ()))
NN = (((1,), (0,)), ((), ()))


def matmul(left, right, dims=NN):
    return lax.dot_general(left, right, dims, preferred_element_type=jnp.float32)


def to_lanes(columns):
    rows = columns.shape[0]
    square = jnp.concatenate([columns, jnp.zeros((128 - rows, 128), jnp.float32)], axis=0)
    return jnp.transpose(square)[:8]


def to_columns(lanes, rows):
    square = jnp.concatenate([lanes, jnp.zeros((120, 128), jnp.float32)], axis=0)
    return jnp.transpose(square)[:rows]


def spread(per_head, width):
    rows = per_head.shape[0]
    owner = lax.broadcasted_iota(jnp.int32, (rows, width), 1) // KV
    result = jnp.zeros((rows, width), jnp.float32)
    for head in range(width // KV):
        result = jnp.where(owner == head, per_head[:, head : head + 1], result)
    return result


def attend(queries, keys, values, first_query):
    rows, width = queries.shape
    heads = width // KV
    owner = lax.broadcasted_iota(jnp.int32, (rows, width), 1) // KV
    zero = jnp.zeros_like(queries)
    stacked = jnp.concatenate(
        [jnp.where(owner == head, queries, zero) for head in range(heads)], axis=0
    )
    scores = matmul(stacked, keys, NT)
    if first_query is not None:
        token = lax.broadcasted_iota(jnp.int32, (rows, scores.shape[1]), 0) + first_query
        seen = lax.broadcasted_iota(jnp.int32, (rows, scores.shape[1]), 1) <= token
        scores = jnp.where(
            jnp.concatenate([seen] * heads, axis=0), scores, jnp.float32(-1e30)
        )
    peak = jnp.max(scores, axis=1, keepdims=True)
    weights = jnp.exp(scores - peak)
    total = jnp.sum(weights, axis=1, keepdims=True)
    mixed = matmul(weights.astype(jnp.bfloat16), values)
    mixed = mixed / total
    level = peak + jnp.log(total)
    result = jnp.zeros((rows, width), jnp.float32)
    levels = jnp.zeros((rows, 128), jnp.float32)
    column = lax.broadcasted_iota(jnp.int32, (rows, 128), 1)
    for head in range(heads):
        part = slice(head * rows, (head + 1) * rows)
        result = jnp.where(owner == head, mixed[part], result)
        levels = jnp.where(column == head, level[part], levels)
    return result, levels


def place_gather(buffer, send, recv, position, sizes, device_of):
    x, l, core = position
    x_size, device_count = sizes
    own = x * 4 + l * 2 + core
    across = x * 4 + (1 - l) * 2 + core
    sibling = device_of(x * 4 + l * 2 + 1 - core)
    partner = device_of(across)

    def slot_at(step, pair):
        return lax.rem(x + step, x_size) * 4 + pair * 2 + core

    def copy(slot, sender, device):
        return pltpu.make_async_remote_copy(
            src_ref=buffer(slot),
            dst_ref=buffer(slot),
            send_sem=send.at[sender],
            recv_sem=recv.at[slot],
            device_id=device,
            device_id_type=MESH,
        )

    def arrived(slot):
        copy(slot, 0, sibling).wait_recv()

    def to_sibling(slot, sender):
        copy(slot, sender, sibling).start()

    def to_partner(slot, sender):
        copy(slot, sender, partner).start()

    def to_line(slot, sender):
        each(1, x_size, lambda step: copy(slot, sender + step, device_of(slot_at(step, l))).start())

    class Gather:
        @staticmethod
        def start():
            to_partner(own, 0)
            to_sibling(own, 1)

        @staticmethod
        def start_line():
            to_line(own, 1)

        @staticmethod
        def middle():
            arrived(across)
            to_line(across, x_size)
            to_sibling(across, 2 * x_size)

        @staticmethod
        def forward():
            def one(step):
                arrived(slot_at(step, l))
                to_sibling(slot_at(step, l), 2 * x_size + step)

            each(1, x_size, one)

        @staticmethod
        def forward_across():
            def one(step):
                arrived(slot_at(step, 1 - l))
                to_sibling(slot_at(step, 1 - l), 3 * x_size - 1 + step)

            each(1, x_size, one)

        @staticmethod
        def finish():
            each(0, device_count // 2, lambda step: arrived(step * 2 + 1 - core))

        @staticmethod
        def drain():
            each(0, 4 * x_size - 1, lambda sender: copy(own, sender, sibling).wait_send())

    return Gather


def each(low, high, step_fn):
    def step(index, carry):
        step_fn(index)
        return carry

    lax.fori_loop(low, high, step, 0)


def kernel(
    planes,
    plane_size,
    head_devices,
    hidden_in,
    self_gain_in,
    cross_gain_in,
    self_query,
    self_key,
    self_value,
    self_out,
    enc_key,
    enc_value,
    cross_query,
    cross_out,
    out,
    hidden,
    self_gain,
    cross_gain,
    weights,
    normed,
    kv,
    qs,
    sent_part,
    sent_level,
    got_part,
    got_level,
    own_part,
    own_level,
    side,
    out_weights,
    query_own,
    query_weights,
    last_own,
    last_weights,
    mixed_rows,
    gained,
    attn_self,
    attn_cross,
    query_terms,
    got_terms,
    squares,
    load_sem,
    kv_send,
    kv_recv,
    side_send,
    side_recv,
    query_send,
    query_recv,
    last_send,
    last_recv,
    side_z_send,
    side_z_recv,
    q_send,
    q_recv,
    part_send,
    part_recv,
    level_send,
    level_recv,
    query_z_send,
    query_z_recv,
    last_z_send,
    last_z_recv,
    query_y_send,
    query_y_recv,
    last_y_send,
    last_y_recv,
    so_y_send,
    so_y_recv,
    so_c_send,
    so_c_recv,
    self_send,
    self_recv,
    cross_send,
    cross_recv,
    terms_send,
    terms_recv,
    square_send,
    square_recv,
):
    rows, width = hidden.shape
    share = width // head_devices
    x_size = plane_size // 4
    ctx = lax.axis_index("ctx")
    head = lax.axis_index("head")
    plane = ctx // plane_size
    place = ctx % plane_size
    position = (place // 4, (place // 2) % 2, place % 2)
    per_head = planes // head_devices
    columns = pl.ds(pl.multiple_of(head * share, share), share)

    def in_plane(other_place):
        return (plane * plane_size + other_place, head)

    def on_line(other_plane):
        return (other_plane * plane_size + place, head)

    def line_plane(step):
        return (plane + step) % planes

    def head_at(step):
        return (head + step) % head_devices

    def remote(src, dst, send, recv, device):
        return pltpu.make_async_remote_copy(
            src_ref=src,
            dst_ref=dst,
            send_sem=send,
            recv_sem=recv,
            device_id=device,
            device_id_type=MESH,
        )

    barrier = pltpu.get_barrier_semaphore()

    def greet(device):
        pl.semaphore_signal(barrier, inc=1, device_id=device, device_id_type=MESH)

    x, l, core = position

    def line_place(step):
        return lax.rem(x + step, x_size) * 4 + l * 2 + core

    each(1, x_size, lambda step: greet(in_plane(line_place(step))))
    greet(in_plane(x * 4 + (1 - l) * 2 + core))
    greet(in_plane(x * 4 + l * 2 + 1 - core))
    each(1, planes, lambda step: greet(on_line(line_plane(step))))
    each(1, head_devices, lambda step: greet((ctx, head_at(step))))

    loads = [
        pltpu.make_async_copy(source, target, load_sem.at[index])
        for index, (source, target) in enumerate(
            (
                (hidden_in, hidden),
                (self_gain_in, self_gain),
                (self_key, weights.at[0]),
                (self_value, weights.at[1]),
                (self_query, weights.at[2]),
                (self_out.at[head], out_weights.at[head]),
                (enc_key, side.at[0, plane, place]),
                (enc_value, side.at[1, plane, place]),
                (cross_query, query_own),
                (cross_out, last_own),
                (cross_gain_in, cross_gain),
            )
        )
    ]
    for load in loads[:5]:
        load.start()

    loads[0].wait()
    loads[1].wait()
    inputs = hidden[...].astype(jnp.float32)
    mean_square = jnp.mean(inputs * inputs, axis=1, keepdims=True)
    normed[...] = (inputs * lax.rsqrt(mean_square + epsilon) * self_gain[...]).astype(jnp.bfloat16)
    for load in loads[5:]:
        load.start()
    for index in range(2):
        loads[2 + index].wait()
        kv[index, place] = matmul(normed[...], weights[index]).astype(jnp.bfloat16)

    pl.semaphore_wait(barrier, (x_size - 1) + 2 + (planes - 1) + (head_devices - 1))

    sizes = (x_size, plane_size)
    kv_pair = place_gather(
        lambda slot: kv.at[:, slot], kv_send, kv_recv, position, sizes, in_plane
    )
    side_pair = place_gather(
        lambda slot: side.at[:, :, slot], side_send, side_recv, position, sizes, in_plane
    )
    query_pair = place_gather(
        lambda slot: query_weights.at[:, :, slot], query_send, query_recv, position, sizes, in_plane
    )
    last_pair = place_gather(
        lambda slot: last_weights.at[:, :, slot], last_send, last_recv, position, sizes, in_plane
    )

    def query_copy(source_plane, target_plane):
        return remote(
            qs.at[source_plane],
            qs.at[source_plane],
            q_send.at[target_plane],
            q_recv.at[source_plane],
            on_line(target_plane),
        )

    def side_line(step, other):
        block = side.at[:, other, place]
        return remote(
            block, block, side_z_send.at[step], side_z_recv.at[other], on_line(line_plane(step))
        )

    def so_heads(source, target):
        return remote(
            self_out.at[target, core],
            out_weights.at[source, core],
            so_y_send.at[target],
            so_y_recv.at[source],
            (ctx, target),
        )

    def so_sibling(source, half):
        block = out_weights.at[source, half]
        return remote(
            block, block, so_c_send.at[source], so_c_recv.at[source], in_plane(x * 4 + l * 2 + 1 - core)
        )

    def by_features(buffer, own, y_send, y_recv, z_send, z_recv):
        target = plane // per_head
        slot = plane % per_head

        def to_head(source, other):
            return remote(
                own, buffer.at[slot, source, place], y_send.at[0], y_recv.at[source], (ctx, other)
            )

        def line(step, which):
            block = buffer.at[which, :, place]
            return remote(block, block, z_send.at[step], z_recv.at[which], on_line(line_plane(step)))

        def start():
            @pl.when(head != target)
            def _():
                to_head(head, target).start()

        def start_line():
            @pl.when(head == target)
            def _():
                buffer[slot, head, place] = own[...]
                each(1, head_devices, lambda step: to_head(head_at(step), head).wait_recv())
                each(1, planes, lambda step: line(step, slot).start())

        def finish():
            def arrival(which):
                @pl.when(plane != head * per_head + which)
                def _():
                    line(1, which).wait_recv()

            each(0, per_head, arrival)

        def drain():
            @pl.when(head != target)
            def _():
                to_head(head, target).wait_send()

            @pl.when(head == target)
            def _():
                each(1, planes, lambda step: line(step, slot).wait_send())

        return start, start_line, finish, drain

    query_start, query_line, query_finish, query_drain = by_features(
        query_weights, query_own, query_y_send, query_y_recv, query_z_send, query_z_recv
    )
    last_start, last_line, last_finish, last_drain = by_features(
        last_weights, last_own, last_y_send, last_y_recv, last_z_send, last_z_recv
    )

    kv_pair.start()
    kv_pair.start_line()
    for load in loads[5:]:
        load.wait()
    query_start()
    last_start()
    each(1, planes, lambda step: side_line(step, plane).start())
    loads[4].wait()
    qs[plane] = matmul(normed[...], weights[2]).astype(jnp.bfloat16)
    each(0, plane, lambda target: query_copy(plane, target).start())
    each(1, head_devices, lambda step: so_heads(head, head_at(step)).start())
    kv_pair.middle()
    query_line()
    last_line()
    kv_pair.forward()
    kv_pair.forward_across()
    kv_pair.finish()

    each(1, planes, lambda step: side_line(step, line_plane(step)).wait_recv())
    side_pair.start()
    side_pair.start_line()

    key_count = plane_size * rows
    hc = qs.shape[2]

    def part_copy(source_plane, target_plane):
        return remote(
            sent_part.at[target_plane],
            got_part.at[source_plane],
            part_send.at[target_plane],
            part_recv.at[source_plane],
            on_line(target_plane),
        )

    def level_copy(source_plane, target_plane):
        return remote(
            sent_level.at[target_plane],
            got_level.at[source_plane],
            level_send.at[target_plane],
            level_recv.at[source_plane],
            on_line(target_plane),
        )

    each(plane + 1, planes, lambda other: query_copy(other, plane).wait_recv())

    def later_planes(low, high):
        for step in reversed(range(low, high)):
            other = line_plane(step)
            part, levels = attend(
                qs[other], kv[0].reshape(key_count, hc), kv[1].reshape(key_count, hc), None
            )
            sent_part[other] = part.astype(jnp.bfloat16)
            sent_level[other] = to_lanes(levels)

        def send(step):
            part_copy(plane, plane + step).start()
            level_copy(plane, plane + step).start()

        each(low, jnp.minimum(high, planes - plane), send)

    half = planes // 2

    if half > 1:

        @pl.when(plane < half)
        def _():
            later_planes(half, planes)

    query_finish()
    query_pair.start()
    query_pair.start_line()

    later_planes(1, half if half > 1 else planes)
    part, levels = attend(
        qs[plane], kv[0].reshape(key_count, hc), kv[1].reshape(key_count, hc), place * rows
    )
    own_part[...] = part
    own_level[...] = levels

    query_pair.middle()
    side_pair.middle()
    last_finish()
    last_pair.start()
    last_pair.start_line()

    def so_arrival(step):
        other = head_at(step)
        so_heads(other, head).wait_recv()
        so_sibling(other, core).start()

    each(1, head_devices, so_arrival)

    def join(other, state):
        mixed, peak, total = state
        part_copy(other, plane).wait_recv()
        level_copy(other, plane).wait_recv()
        level = to_columns(got_level[other], rows)
        new_peak = jnp.maximum(peak, level)
        keep = jnp.exp(peak - new_peak)
        add = jnp.exp(level - new_peak)
        mixed = mixed * spread(keep, hc) + got_part[other].astype(jnp.float32) * spread(add, hc)
        return mixed, new_peak, total * keep + add

    mixed, _, total = lax.fori_loop(
        0, plane, join, (own_part[...], own_level[...], jnp.ones((rows, 128), jnp.float32))
    )
    attn_self[head] = (mixed / spread(total, hc)).astype(jnp.bfloat16)

    farthest_first = sorted(
        range(1, head_devices), key=lambda step: -min(step, head_devices - step)
    )

    def exchange(buffer, send, recv):
        def copy(slot, step):
            return remote(
                buffer.at[slot],
                buffer.at[slot],
                send.at[step],
                recv.at[slot],
                (ctx, head_at(step)),
            )

        def start():
            for step in farthest_first:
                copy(head, step).start()

        def finish(step):
            copy(head_at(step), step).wait_recv()

        def drain():
            each(1, head_devices, lambda step: copy(head, step).wait_send())

        return start, finish, drain

    self_start, self_finish, self_drain = exchange(attn_self, self_send, self_recv)
    self_start()
    last_pair.middle()
    query_pair.forward()
    side_pair.forward()
    each(1, head_devices, lambda step: so_sibling(head_at(step), 1 - core).wait_recv())

    def self_term(step):
        other = head_at(step)
        return matmul(attn_self[other], out_weights[other].reshape(share, hc), NT)

    mixed = hidden[:, columns].astype(jnp.float32) + self_term(0)
    for step in reversed(farthest_first):
        self_finish(step)
        mixed = mixed + self_term(step)
    mixed_rows[...] = mixed

    square = jnp.sum(mixed * mixed, axis=1, keepdims=True)
    squares[head] = to_lanes(jnp.broadcast_to(square, (rows, 128)))
    square_start, square_finish, square_drain = exchange(squares, square_send, square_recv)
    square_start()
    gained[...] = (mixed * cross_gain[:, columns]).astype(jnp.bfloat16)
    query_pair.forward_across()
    query_pair.finish()
    piece_rows = share // per_head

    def query_term(other):
        return sum(
            matmul(
                gained[:, slot * piece_rows : (slot + 1) * piece_rows],
                query_weights[slot, other].reshape(piece_rows, hc),
            )
            for slot in range(per_head)
        )

    def term_copy(step, slot):
        other = head_at(step)
        return remote(
            query_terms.at[other],
            got_terms.at[slot],
            terms_send.at[step],
            terms_recv.at[slot],
            (ctx, other),
        )

    for step in farthest_first:
        query_terms[head_at(step)] = query_term(head_at(step)).astype(jnp.bfloat16)
        term_copy(step, head).start()
    cross_q = query_term(head)

    side_pair.forward_across()
    last_pair.forward()
    side_pair.finish()
    all_squares = squares[head]
    for step in range(1, head_devices):
        square_finish(step)
        all_squares = all_squares + squares[head_at(step)]
        term_copy(step, head_at(step)).wait_recv()
        cross_q = cross_q + got_terms[head_at(step)].astype(jnp.float32)
    scale = lax.rsqrt(to_columns(all_squares, rows)[:, :1] / width + epsilon)
    cross_q = (cross_q * scale).astype(jnp.bfloat16)

    side_rows = planes * plane_size * side.shape[3]
    crossed, _ = attend(
        cross_q, side[0].reshape(side_rows, hc), side[1].reshape(side_rows, hc), None
    )
    attn_cross[head] = crossed.astype(jnp.bfloat16)
    cross_start, cross_finish, cross_drain = exchange(attn_cross, cross_send, cross_recv)
    cross_start()
    last_pair.forward_across()
    last_pair.finish()

    result = mixed_rows[...]
    for step in [0, *reversed(farthest_first)]:
        if step:
            cross_finish(step)
        other = head_at(step)
        terms = [
            matmul(
                attn_cross[other],
                last_weights[slot, other].reshape(share // per_head, hc),
                NT,
            )
            for slot in range(per_head)
        ]
        result = result + jnp.concatenate(terms, axis=1)
    out[...] = result.astype(jnp.bfloat16)

    each(1, planes, lambda step: side_line(step, plane).wait_send())
    each(1, head_devices, lambda step: so_heads(head, head_at(step)).wait_send())
    each(1, head_devices, lambda step: so_sibling(head_at(step), core).wait_send())
    query_drain()
    last_drain()
    kv_pair.drain()
    side_pair.drain()
    query_pair.drain()
    last_pair.drain()
    each(0, plane, lambda target: query_copy(plane, target).wait_send())
    each(plane + 1, planes, lambda other: part_copy(plane, other).wait_send())
    each(plane + 1, planes, lambda other: level_copy(plane, other).wait_send())
    self_drain()
    cross_drain()
    square_drain()
    each(1, head_devices, lambda step: term_copy(step, head).wait_send())


def body(
    plane_size,
    hidden,
    self_gain,
    cross_gain,
    self_query,
    self_key,
    self_value,
    self_out,
    cross_query,
    cross_out,
    enc_key,
    enc_value,
):
    rows, width = hidden.shape
    hc = self_query.shape[1]
    ctx_devices = lax.axis_size("ctx")
    head_devices = lax.axis_size("head")
    planes = ctx_devices // plane_size
    share = width // head_devices
    piece = enc_key.shape[0]
    low, full = jnp.bfloat16, jnp.float32
    vmem = pl.BlockSpec(memory_space=pltpu.VMEM)
    hbm = pl.BlockSpec(memory_space=pl.ANY)
    dma = pltpu.SemaphoreType.DMA
    return pl.pallas_call(
        functools.partial(kernel, planes, plane_size, head_devices),
        out_shape=jax.ShapeDtypeStruct((rows, share), low),
        in_specs=[hbm] * 11,
        out_specs=vmem,
        scratch_shapes=[
            pltpu.VMEM((rows, width), low),
            pltpu.VMEM((1, width), full),
            pltpu.VMEM((1, width), full),
            pltpu.VMEM((3, width, hc), low),
            pltpu.VMEM((rows, width), low),
            pltpu.VMEM((2, plane_size, rows, hc), low),
            pltpu.VMEM((planes, rows, hc), low),
            pltpu.VMEM((planes, rows, hc), low),
            pltpu.VMEM((planes, 8, 128), full),
            pltpu.VMEM((planes, rows, hc), low),
            pltpu.VMEM((planes, 8, 128), full),
            pltpu.VMEM((rows, hc), full),
            pltpu.VMEM((rows, 128), full),
            pltpu.VMEM((2, planes, plane_size, piece, hc), low),
            pltpu.VMEM((head_devices, 2, share // 2, hc), low),
            pltpu.VMEM((piece, hc), low),
            pltpu.VMEM((planes // head_devices, head_devices, plane_size, piece, hc), low),
            pltpu.VMEM((piece, hc), low),
            pltpu.VMEM((planes // head_devices, head_devices, plane_size, piece, hc), low),
            pltpu.VMEM((rows, share), full),
            pltpu.VMEM((rows, share), low),
            pltpu.VMEM((head_devices, rows, hc), low),
            pltpu.VMEM((head_devices, rows, hc), low),
            pltpu.VMEM((head_devices, rows, hc), low),
            pltpu.VMEM((head_devices, rows, hc), low),
            pltpu.VMEM((head_devices, 8, 128), full),
            dma((11,)),
        ]
        + [dma((plane_size,))] * 8
        + [dma((planes,))] * 12
        + [dma((head_devices,))] * 16,
        compiler_params=pltpu.CompilerParams(
            collective_id=0, has_side_effects=True, vmem_limit_bytes=VMEM_BYTES
        ),
    )(
        hidden,
        self_gain.reshape(1, width),
        cross_gain.reshape(1, width),
        self_query,
        self_key,
        self_value,
        self_out.reshape(head_devices, 2, share // 2, hc),
        enc_key,
        enc_value,
        cross_query,
        cross_out,
    )


def solution(mesh, plane_size=PLANE):
    placed = (
        P("ctx", None),
        P(),
        P(),
        P(None, "head"),
        P(None, "head"),
        P(None, "head"),
        P(None, "head"),
        P("ctx", "head"),
        P("ctx", "head"),
        P("ctx", "head"),
        P("ctx", "head"),
    )
    return jax.shard_map(
        functools.partial(body, plane_size),
        mesh=mesh,
        in_specs=placed,
        out_specs=P("ctx", "head"),
        check_vma=False,
    )
```

```python
import functools

import jax
import jax.numpy as jnp
from jax import lax
from jax.experimental import pallas as pl
from jax.experimental.pallas import tpu as pltpu
from jax.sharding import PartitionSpec as P

KV = 64
PLANE = 16
VMEM_BYTES = 62 * 1024 * 1024
MESH = pl.DeviceIdType.MESH

epsilon = 1e-06

NT = (((1,), (1,)), ((), ()))
NN = (((1,), (0,)), ((), ()))


def matmul(left, right, dims=NN):
    return lax.dot_general(left, right, dims, preferred_element_type=jnp.float32)


def to_lanes(columns):
    rows = columns.shape[0]
    square = jnp.concatenate([columns, jnp.zeros((128 - rows, 128), jnp.float32)], axis=0)
    return jnp.transpose(square)[:8]


def to_columns(lanes, rows):
    square = jnp.concatenate([lanes, jnp.zeros((120, 128), jnp.float32)], axis=0)
    return jnp.transpose(square)[:rows]


def spread(per_head, width):
    rows = per_head.shape[0]
    owner = lax.broadcasted_iota(jnp.int32, (rows, width), 1) // KV
    result = jnp.zeros((rows, width), jnp.float32)
    for head in range(width // KV):
        result = jnp.where(owner == head, per_head[:, head : head + 1], result)
    return result


def attend(queries, keys, values, first_query):
    rows, width = queries.shape
    heads = width // KV
    owner = lax.broadcasted_iota(jnp.int32, (rows, width), 1) // KV
    zero = jnp.zeros_like(queries)
    stacked = jnp.concatenate(
        [jnp.where(owner == head, queries, zero) for head in range(heads)], axis=0
    )
    scores = matmul(stacked, keys, NT)
    if first_query is not None:
        token = lax.broadcasted_iota(jnp.int32, (rows, scores.shape[1]), 0) + first_query
        seen = lax.broadcasted_iota(jnp.int32, (rows, scores.shape[1]), 1) <= token
        scores = jnp.where(
            jnp.concatenate([seen] * heads, axis=0), scores, jnp.float32(-1e30)
        )
    peak = jnp.max(scores, axis=1, keepdims=True)
    weights = jnp.exp(scores - peak)
    total = jnp.sum(weights, axis=1, keepdims=True)
    mixed = matmul(weights.astype(jnp.bfloat16), values)
    mixed = mixed / total
    level = peak + jnp.log(total)
    result = jnp.zeros((rows, width), jnp.float32)
    levels = jnp.zeros((rows, 128), jnp.float32)
    column = lax.broadcasted_iota(jnp.int32, (rows, 128), 1)
    for head in range(heads):
        part = slice(head * rows, (head + 1) * rows)
        result = jnp.where(owner == head, mixed[part], result)
        levels = jnp.where(column == head, level[part], levels)
    return result, levels


def place_gather(buffer, send, recv, position, sizes, device_of):
    x, l, core = position
    x_size, device_count = sizes
    own = x * 4 + l * 2 + core
    across = x * 4 + (1 - l) * 2 + core
    sibling = device_of(x * 4 + l * 2 + 1 - core)
    partner = device_of(across)

    def slot_at(step, pair):
        return lax.rem(x + step, x_size) * 4 + pair * 2 + core

    def copy(slot, sender, device):
        return pltpu.make_async_remote_copy(
            src_ref=buffer(slot),
            dst_ref=buffer(slot),
            send_sem=send.at[sender],
            recv_sem=recv.at[slot],
            device_id=device,
            device_id_type=MESH,
        )

    def arrived(slot):
        copy(slot, 0, sibling).wait_recv()

    def to_sibling(slot, sender):
        copy(slot, sender, sibling).start()

    def to_partner(slot, sender):
        copy(slot, sender, partner).start()

    def to_line(slot, sender):
        for step in sorted(range(1, x_size), key=lambda step: -min(step, x_size - step)):
            copy(slot, sender + step, device_of(slot_at(step, l))).start()

    class Gather:
        @staticmethod
        def start():
            to_partner(own, 0)
            to_sibling(own, 1)

        @staticmethod
        def start_line():
            to_line(own, 1)

        @staticmethod
        def middle():
            arrived(across)
            to_line(across, x_size)
            to_sibling(across, 2 * x_size)

        @staticmethod
        def forward():
            def one(step):
                arrived(slot_at(step, l))
                to_sibling(slot_at(step, l), 2 * x_size + step)

            each(1, x_size, one)

        @staticmethod
        def forward_across():
            def one(step):
                arrived(slot_at(step, 1 - l))
                to_sibling(slot_at(step, 1 - l), 3 * x_size - 1 + step)

            each(1, x_size, one)

        @staticmethod
        def finish():
            each(0, device_count // 2, lambda step: arrived(step * 2 + 1 - core))

        @staticmethod
        def drain():
            each(0, 4 * x_size - 1, lambda sender: copy(own, sender, sibling).wait_send())

    return Gather


def each(low, high, step_fn):
    def step(index, carry):
        step_fn(index)
        return carry

    lax.fori_loop(low, high, step, 0)


def kernel(
    planes,
    plane_size,
    head_devices,
    hidden_in,
    self_gain_in,
    cross_gain_in,
    self_query,
    self_key,
    self_value,
    self_out,
    enc_key,
    enc_value,
    cross_query,
    cross_out,
    out,
    hidden,
    self_gain,
    cross_gain,
    weights,
    normed,
    kv,
    qs,
    sent_part,
    sent_level,
    got_part,
    got_level,
    own_part,
    own_level,
    side,
    out_weights,
    query_own,
    query_weights,
    last_own,
    last_weights,
    mixed_rows,
    gained,
    attn_self,
    attn_cross,
    query_terms,
    got_terms,
    squares,
    load_sem,
    kv_send,
    kv_recv,
    side_send,
    side_recv,
    query_send,
    query_recv,
    last_send,
    last_recv,
    side_z_send,
    side_z_recv,
    q_send,
    q_recv,
    part_send,
    part_recv,
    level_send,
    level_recv,
    query_z_send,
    query_z_recv,
    last_z_send,
    last_z_recv,
    query_y_send,
    query_y_recv,
    last_y_send,
    last_y_recv,
    so_y_send,
    so_y_recv,
    so_c_send,
    so_c_recv,
    self_send,
    self_recv,
    cross_send,
    cross_recv,
    terms_send,
    terms_recv,
    square_send,
    square_recv,
):
    rows, width = hidden.shape
    share = width // head_devices
    x_size = plane_size // 4
    ctx = lax.axis_index("ctx")
    head = lax.axis_index("head")
    plane = ctx // plane_size
    place = ctx % plane_size
    position = (place // 4, (place // 2) % 2, place % 2)
    per_head = planes // head_devices
    columns = pl.ds(pl.multiple_of(head * share, share), share)

    def in_plane(other_place):
        return (plane * plane_size + other_place, head)

    def on_line(other_plane):
        return (other_plane * plane_size + place, head)

    def line_plane(step):
        return (plane + step) % planes

    def head_at(step):
        return (head + step) % head_devices

    def remote(src, dst, send, recv, device):
        return pltpu.make_async_remote_copy(
            src_ref=src,
            dst_ref=dst,
            send_sem=send,
            recv_sem=recv,
            device_id=device,
            device_id_type=MESH,
        )

    barrier = pltpu.get_barrier_semaphore()

    def greet(device):
        pl.semaphore_signal(barrier, inc=1, device_id=device, device_id_type=MESH)

    x, l, core = position

    def line_place(step):
        return lax.rem(x + step, x_size) * 4 + l * 2 + core

    each(1, x_size, lambda step: greet(in_plane(line_place(step))))
    greet(in_plane(x * 4 + (1 - l) * 2 + core))
    greet(in_plane(x * 4 + l * 2 + 1 - core))
    each(1, planes, lambda step: greet(on_line(line_plane(step))))
    each(1, head_devices, lambda step: greet((ctx, head_at(step))))

    loads = [
        pltpu.make_async_copy(source, target, load_sem.at[index])
        for index, (source, target) in enumerate(
            (
                (hidden_in, hidden),
                (self_gain_in, self_gain),
                (self_key, weights.at[0]),
                (self_value, weights.at[1]),
                (self_query, weights.at[2]),
                (self_out.at[head], out_weights.at[head]),
                (enc_key, side.at[0, plane, place]),
                (enc_value, side.at[1, plane, place]),
                (cross_query, query_own),
                (cross_out, last_own),
                (cross_gain_in, cross_gain),
            )
        )
    ]
    for load in loads[:5]:
        load.start()

    loads[0].wait()
    loads[1].wait()
    inputs = hidden[...].astype(jnp.float32)
    mean_square = jnp.mean(inputs * inputs, axis=1, keepdims=True)
    normed[...] = (inputs * lax.rsqrt(mean_square + epsilon) * self_gain[...]).astype(jnp.bfloat16)
    for load in loads[5:]:
        load.start()
    for index in range(2):
        loads[2 + index].wait()
        kv[index, place] = matmul(normed[...], weights[index]).astype(jnp.bfloat16)

    pl.semaphore_wait(barrier, (x_size - 1) + 2 + (planes - 1) + (head_devices - 1))

    sizes = (x_size, plane_size)
    kv_pair = place_gather(
        lambda slot: kv.at[:, slot], kv_send, kv_recv, position, sizes, in_plane
    )
    side_pair = place_gather(
        lambda slot: side.at[:, :, slot], side_send, side_recv, position, sizes, in_plane
    )
    query_pair = place_gather(
        lambda slot: query_weights.at[:, :, slot], query_send, query_recv, position, sizes, in_plane
    )
    last_pair = place_gather(
        lambda slot: last_weights.at[:, :, slot], last_send, last_recv, position, sizes, in_plane
    )

    def query_copy(source_plane, target_plane):
        return remote(
            qs.at[source_plane],
            qs.at[source_plane],
            q_send.at[target_plane],
            q_recv.at[source_plane],
            on_line(target_plane),
        )

    def side_line(step, other):
        block = side.at[:, other, place]
        return remote(
            block, block, side_z_send.at[step], side_z_recv.at[other], on_line(line_plane(step))
        )

    def so_heads(source, target):
        return remote(
            self_out.at[target, core],
            out_weights.at[source, core],
            so_y_send.at[target],
            so_y_recv.at[source],
            (ctx, target),
        )

    def so_sibling(source, half):
        block = out_weights.at[source, half]
        return remote(
            block, block, so_c_send.at[source], so_c_recv.at[source], in_plane(x * 4 + l * 2 + 1 - core)
        )

    def by_features(buffer, own, y_send, y_recv, z_send, z_recv):
        target = plane // per_head
        slot = plane % per_head

        def to_head(source, other):
            return remote(
                own, buffer.at[slot, source, place], y_send.at[0], y_recv.at[source], (ctx, other)
            )

        def line(step, which):
            block = buffer.at[which, :, place]
            return remote(block, block, z_send.at[step], z_recv.at[which], on_line(line_plane(step)))

        def start():
            @pl.when(head != target)
            def _():
                to_head(head, target).start()

        def start_line():
            @pl.when(head == target)
            def _():
                buffer[slot, head, place] = own[...]
                each(1, head_devices, lambda step: to_head(head_at(step), head).wait_recv())
                each(1, planes, lambda step: line(step, slot).start())

        def finish():
            def arrival(which):
                @pl.when(plane != head * per_head + which)
                def _():
                    line(1, which).wait_recv()

            each(0, per_head, arrival)

        def drain():
            @pl.when(head != target)
            def _():
                to_head(head, target).wait_send()

            @pl.when(head == target)
            def _():
                each(1, planes, lambda step: line(step, slot).wait_send())

        return start, start_line, finish, drain

    query_start, query_line, query_finish, query_drain = by_features(
        query_weights, query_own, query_y_send, query_y_recv, query_z_send, query_z_recv
    )
    last_start, last_line, last_finish, last_drain = by_features(
        last_weights, last_own, last_y_send, last_y_recv, last_z_send, last_z_recv
    )

    kv_pair.start()
    kv_pair.start_line()
    for load in loads[5:]:
        load.wait()
    query_start()
    last_start()
    each(1, planes, lambda step: side_line(step, plane).start())
    loads[4].wait()
    qs[plane] = matmul(normed[...], weights[2]).astype(jnp.bfloat16)
    each(0, plane, lambda target: query_copy(plane, target).start())
    each(1, head_devices, lambda step: so_heads(head, head_at(step)).start())
    kv_pair.middle()
    query_line()
    last_line()
    kv_pair.forward()
    kv_pair.forward_across()
    kv_pair.finish()

    each(1, planes, lambda step: side_line(step, line_plane(step)).wait_recv())
    side_pair.start()
    side_pair.start_line()

    key_count = plane_size * rows
    hc = qs.shape[2]

    def part_copy(source_plane, target_plane):
        return remote(
            sent_part.at[target_plane],
            got_part.at[source_plane],
            part_send.at[target_plane],
            part_recv.at[source_plane],
            on_line(target_plane),
        )

    def level_copy(source_plane, target_plane):
        return remote(
            sent_level.at[target_plane],
            got_level.at[source_plane],
            level_send.at[target_plane],
            level_recv.at[source_plane],
            on_line(target_plane),
        )

    each(plane + 1, planes, lambda other: query_copy(other, plane).wait_recv())

    def later_planes(low, high):
        for step in reversed(range(low, high)):
            other = line_plane(step)
            part, levels = attend(
                qs[other], kv[0].reshape(key_count, hc), kv[1].reshape(key_count, hc), None
            )
            sent_part[other] = part.astype(jnp.bfloat16)
            sent_level[other] = to_lanes(levels)

        def send(step):
            part_copy(plane, plane + step).start()
            level_copy(plane, plane + step).start()

        each(low, jnp.minimum(high, planes - plane), send)

    half = planes // 2

    if half > 1:

        @pl.when(plane < half)
        def _():
            later_planes(half, planes)

    query_finish()
    query_pair.start()
    query_pair.start_line()

    later_planes(1, half if half > 1 else planes)
    part, levels = attend(
        qs[plane], kv[0].reshape(key_count, hc), kv[1].reshape(key_count, hc), place * rows
    )
    own_part[...] = part
    own_level[...] = levels

    query_pair.middle()
    side_pair.middle()
    last_finish()
    last_pair.start()
    last_pair.start_line()

    def so_arrival(step):
        other = head_at(step)
        so_heads(other, head).wait_recv()
        so_sibling(other, core).start()

    each(1, head_devices, so_arrival)

    def join(other, state):
        mixed, peak, total = state
        part_copy(other, plane).wait_recv()
        level_copy(other, plane).wait_recv()
        level = to_columns(got_level[other], rows)
        new_peak = jnp.maximum(peak, level)
        keep = jnp.exp(peak - new_peak)
        add = jnp.exp(level - new_peak)
        mixed = mixed * spread(keep, hc) + got_part[other].astype(jnp.float32) * spread(add, hc)
        return mixed, new_peak, total * keep + add

    mixed, _, total = lax.fori_loop(
        0, plane, join, (own_part[...], own_level[...], jnp.ones((rows, 128), jnp.float32))
    )
    attn_self[head] = (mixed / spread(total, hc)).astype(jnp.bfloat16)

    farthest_first = sorted(
        range(1, head_devices), key=lambda step: -min(step, head_devices - step)
    )

    def exchange(buffer, send, recv):
        def copy(slot, step):
            return remote(
                buffer.at[slot],
                buffer.at[slot],
                send.at[step],
                recv.at[slot],
                (ctx, head_at(step)),
            )

        def start():
            for step in farthest_first:
                copy(head, step).start()

        def finish(step):
            copy(head_at(step), step).wait_recv()

        def drain():
            each(1, head_devices, lambda step: copy(head, step).wait_send())

        return start, finish, drain

    self_start, self_finish, self_drain = exchange(attn_self, self_send, self_recv)
    self_start()
    last_pair.middle()
    query_pair.forward()
    side_pair.forward()
    each(1, head_devices, lambda step: so_sibling(head_at(step), 1 - core).wait_recv())

    def self_term(step):
        other = head_at(step)
        return matmul(attn_self[other], out_weights[other].reshape(share, hc), NT)

    mixed = hidden[:, columns].astype(jnp.float32) + self_term(0)
    for step in reversed(farthest_first):
        self_finish(step)
        mixed = mixed + self_term(step)
    mixed_rows[...] = mixed

    square = jnp.sum(mixed * mixed, axis=1, keepdims=True)
    squares[head] = to_lanes(jnp.broadcast_to(square, (rows, 128)))
    square_start, square_finish, square_drain = exchange(squares, square_send, square_recv)
    square_start()
    gained[...] = (mixed * cross_gain[:, columns]).astype(jnp.bfloat16)
    query_pair.forward_across()
    query_pair.finish()
    piece_rows = share // per_head

    def query_term(other):
        return sum(
            matmul(
                gained[:, slot * piece_rows : (slot + 1) * piece_rows],
                query_weights[slot, other].reshape(piece_rows, hc),
            )
            for slot in range(per_head)
        )

    def term_copy(step, slot):
        other = head_at(step)
        return remote(
            query_terms.at[other],
            got_terms.at[slot],
            terms_send.at[step],
            terms_recv.at[slot],
            (ctx, other),
        )

    for step in farthest_first:
        query_terms[head_at(step)] = query_term(head_at(step)).astype(jnp.bfloat16)
        term_copy(step, head).start()
    cross_q = query_term(head)

    side_pair.forward_across()
    last_pair.forward()
    side_pair.finish()
    all_squares = squares[head]
    for step in range(1, head_devices):
        square_finish(step)
        all_squares = all_squares + squares[head_at(step)]
        term_copy(step, head_at(step)).wait_recv()
        cross_q = cross_q + got_terms[head_at(step)].astype(jnp.float32)
    scale = lax.rsqrt(to_columns(all_squares, rows)[:, :1] / width + epsilon)
    cross_q = (cross_q * scale).astype(jnp.bfloat16)

    side_rows = planes * plane_size * side.shape[3]
    crossed, _ = attend(
        cross_q, side[0].reshape(side_rows, hc), side[1].reshape(side_rows, hc), None
    )
    attn_cross[head] = crossed.astype(jnp.bfloat16)
    cross_start, cross_finish, cross_drain = exchange(attn_cross, cross_send, cross_recv)
    cross_start()
    last_pair.forward_across()
    last_pair.finish()

    result = mixed_rows[...]
    for step in [0, *reversed(farthest_first)]:
        if step:
            cross_finish(step)
        other = head_at(step)
        terms = [
            matmul(
                attn_cross[other],
                last_weights[slot, other].reshape(share // per_head, hc),
                NT,
            )
            for slot in range(per_head)
        ]
        result = result + jnp.concatenate(terms, axis=1)
    out[...] = result.astype(jnp.bfloat16)

    each(1, planes, lambda step: side_line(step, plane).wait_send())
    each(1, head_devices, lambda step: so_heads(head, head_at(step)).wait_send())
    each(1, head_devices, lambda step: so_sibling(head_at(step), core).wait_send())
    query_drain()
    last_drain()
    kv_pair.drain()
    side_pair.drain()
    query_pair.drain()
    last_pair.drain()
    each(0, plane, lambda target: query_copy(plane, target).wait_send())
    each(plane + 1, planes, lambda other: part_copy(plane, other).wait_send())
    each(plane + 1, planes, lambda other: level_copy(plane, other).wait_send())
    self_drain()
    cross_drain()
    square_drain()
    each(1, head_devices, lambda step: term_copy(step, head).wait_send())


def body(
    plane_size,
    hidden,
    self_gain,
    cross_gain,
    self_query,
    self_key,
    self_value,
    self_out,
    cross_query,
    cross_out,
    enc_key,
    enc_value,
):
    rows, width = hidden.shape
    hc = self_query.shape[1]
    ctx_devices = lax.axis_size("ctx")
    head_devices = lax.axis_size("head")
    planes = ctx_devices // plane_size
    share = width // head_devices
    piece = enc_key.shape[0]
    low, full = jnp.bfloat16, jnp.float32
    vmem = pl.BlockSpec(memory_space=pltpu.VMEM)
    hbm = pl.BlockSpec(memory_space=pl.ANY)
    dma = pltpu.SemaphoreType.DMA
    return pl.pallas_call(
        functools.partial(kernel, planes, plane_size, head_devices),
        out_shape=jax.ShapeDtypeStruct((rows, share), low),
        in_specs=[hbm] * 11,
        out_specs=vmem,
        scratch_shapes=[
            pltpu.VMEM((rows, width), low),
            pltpu.VMEM((1, width), full),
            pltpu.VMEM((1, width), full),
            pltpu.VMEM((3, width, hc), low),
            pltpu.VMEM((rows, width), low),
            pltpu.VMEM((2, plane_size, rows, hc), low),
            pltpu.VMEM((planes, rows, hc), low),
            pltpu.VMEM((planes, rows, hc), low),
            pltpu.VMEM((planes, 8, 128), full),
            pltpu.VMEM((planes, rows, hc), low),
            pltpu.VMEM((planes, 8, 128), full),
            pltpu.VMEM((rows, hc), full),
            pltpu.VMEM((rows, 128), full),
            pltpu.VMEM((2, planes, plane_size, piece, hc), low),
            pltpu.VMEM((head_devices, 2, share // 2, hc), low),
            pltpu.VMEM((piece, hc), low),
            pltpu.VMEM((planes // head_devices, head_devices, plane_size, piece, hc), low),
            pltpu.VMEM((piece, hc), low),
            pltpu.VMEM((planes // head_devices, head_devices, plane_size, piece, hc), low),
            pltpu.VMEM((rows, share), full),
            pltpu.VMEM((rows, share), low),
            pltpu.VMEM((head_devices, rows, hc), low),
            pltpu.VMEM((head_devices, rows, hc), low),
            pltpu.VMEM((head_devices, rows, hc), low),
            pltpu.VMEM((head_devices, rows, hc), low),
            pltpu.VMEM((head_devices, 8, 128), full),
            dma((11,)),
        ]
        + [dma((plane_size,))] * 8
        + [dma((planes,))] * 12
        + [dma((head_devices,))] * 16,
        compiler_params=pltpu.CompilerParams(
            collective_id=0, has_side_effects=True, vmem_limit_bytes=VMEM_BYTES
        ),
    )(
        hidden,
        self_gain.reshape(1, width),
        cross_gain.reshape(1, width),
        self_query,
        self_key,
        self_value,
        self_out.reshape(head_devices, 2, share // 2, hc),
        enc_key,
        enc_value,
        cross_query,
        cross_out,
    )


def solution(mesh, plane_size=PLANE):
    placed = (
        P("ctx", None),
        P(),
        P(),
        P(None, "head"),
        P(None, "head"),
        P(None, "head"),
        P(None, "head"),
        P("ctx", "head"),
        P("ctx", "head"),
        P("ctx", "head"),
        P("ctx", "head"),
    )
    return jax.shard_map(
        functools.partial(body, plane_size),
        mesh=mesh,
        in_specs=placed,
        out_specs=P("ctx", "head"),
        check_vma=False,
    )
```
